256 devices in a mesh: pipe: 16 (over x, y_lo, core), expert: 16 (over z, y_hi).
Axes of the slice: x: 4, y: 4 (y_hi: 2, y_lo: 2; y = y_hi * 2 + y_lo), z: 8, core: 2. Of those that a mesh axis runs over, the one named last changes fastest.
Arguments:
- fwd_rows: bfloat16 [16, 1024, 3584], P('pipe', 'expert'), may hold values from -3 to 3
- fwd_experts: int32 [16, 1024, 2], P('pipe', 'expert'), may hold values from 0 to 3, as said below
- fwd_weight: bfloat16 [16, 1024, 2], P('pipe', 'expert'), may hold values from 0.5 to 1.5
- back_rows: bfloat16 [16, 1024, 3584], P('pipe', 'expert'), may hold values from -3 to 3
- back_experts: int32 [16, 1024, 2], P('pipe', 'expert'), may hold values from 0 to 3, as said below
- back_weight: bfloat16 [16, 1024, 2], P('pipe', 'expert'), may hold values from 0.5 to 1.5
- back_cotangent: bfloat16 [16, 1024, 3584], P('pipe', 'expert'), may hold values from -6 to 6
- norm_gain: bfloat16 [16, 3584], P('pipe'), may hold values from 0.099609375 to 1.8984375
- w_gate: bfloat16 [16, 16, 3584, 256], P('pipe', 'expert'), may hold values from -0.09375 to 0.09375
- w_up: bfloat16 [16, 16, 3584, 256], P('pipe', 'expert'), may hold values from -0.09375 to 0.09375
- w_down: bfloat16 [16, 16, 256, 3584], P('pipe', 'expert'), may hold values from -0.1875 to 0.1875
- saved_gate: bfloat16 [16, 16, 512, 256], P('pipe', 'expert'), may hold values from -6 to 6
- saved_up: bfloat16 [16, 16, 512, 256], P('pipe', 'expert'), may hold values from -6 to 6
Outputs:
- next_input: bfloat16 [16, 1024, 3584], P('pipe', 'expert')
- prev_grad: bfloat16 [16, 1024, 3584], P('pipe', 'expert')
The draws below stay inside these ranges and needn't reach their ends.
Inputs may be any that keep to these rules, and one draw needn't show every extreme that they name: `fwd_experts`: each token names 2 different experts; in every aligned block of 64 tokens each expert is named exactly 32 times. `back_experts`: each token names 2 different experts; in every aligned block of 64 tokens each expert is named exactly 32 times.
All inputs are finite; a program needn't handle non-finite values.
Results may differ from the reference program's by a relative error of at most 0.0065.
Values may be sent and summed in bfloat16 or wider, within the bound.
A program may use at most 64 MiB of HBM per device.

```python
import jax
import jax.numpy as jnp
from jax import lax

D = 3584
FF = 1024
EXPERTS = 4
TOPK = 2
TOK_DEV = 64
SECTIONS = 16
SHARDS = 16
HSPLIT = 4
FF_DEV = 256
CAP = 32
ROWS = 512
TOKENS = 1024


def route_table(key):
    block_count = SECTIONS * (TOKENS // TOK_DEV)
    group_count = TOK_DEV // EXPERTS
    key_perm, key_shift, key_rotate, key_flip = jax.random.split(key, 4)
    perm_keys = jax.random.split(key_perm, block_count)
    ranks = jax.vmap(lambda single: jax.random.permutation(single, TOK_DEV))(perm_keys).astype(jnp.int32)
    shifts = jax.random.randint(key_shift, (block_count, group_count), 1, EXPERTS).astype(jnp.int32)
    rotate = jax.random.randint(key_rotate, (block_count, 1), 0, EXPERTS).astype(jnp.int32)
    flips = jax.random.randint(key_flip, (block_count, TOK_DEV), 0, 2).astype(jnp.int32)
    first = (ranks % EXPERTS + rotate) % EXPERTS
    shift_each = jnp.take_along_axis(shifts, ranks // EXPERTS, axis=1)
    second = (first + shift_each) % EXPERTS
    choice_one = jnp.where(flips == 1, second, first)
    choice_two = jnp.where(flips == 1, first, second)
    table = jnp.stack([choice_one, choice_two], axis=-1)
    return table.reshape(SECTIONS, TOKENS, TOPK).astype(jnp.int32)


def draw_fwd_experts(key, part):
    key = jax.random.fold_in(key, 11)
    return route_table(key)


def draw_back_experts(key, part):
    key = jax.random.fold_in(key, 23)
    return route_table(key)


def block_levels(stream_key, dims, shards, smallest, high):
    def one(dim, shards_of):
        steps = jax.random.uniform(jax.random.fold_in(jax.random.fold_in(stream_key, 6), dim), (shards_of,), jnp.float32, smallest / len(shards), high / len(shards))
        return jnp.repeat(jnp.exp(steps), dims[dim] // shards_of).reshape((-1,) + (1,) * (len(dims) - dim - 1))

    level = one(*shards[0])
    for cut in shards[1:]:
        level = level * one(*cut)
    return level


def gaussian(key, dims, deviation, limit, cuts=(), kind=jnp.bfloat16):
    array = jax.random.normal(key, dims, jnp.float32) * deviation
    if len(cuts) > 0:
        array = block_levels(key, dims, cuts, -0.22, 0.18) * array
    return jnp.clip(array, min=-limit, max=limit).astype(kind)


def setup_inputs(seed: int = 0) -> dict:
    keys = jax.random.split(jax.random.key(seed), 14)
    fwd_rows = gaussian(keys[0], (SECTIONS, TOKENS, D), 0.5, 3.0, ((0, 16), (1, 16)))
    fwd_experts = draw_fwd_experts(jax.random.fold_in(keys[13], 71), 0)
    fwd_weight = jnp.clip(0.5 + 1.0 * jax.random.uniform(keys[2], (SECTIONS, TOKENS, TOPK), jnp.float32) ** block_levels(keys[2], (SECTIONS, TOKENS, TOPK), ((0, 16), (1, 16)), -0.2, 0.2), 0.5, 1.5).astype(jnp.bfloat16)
    back_rows = gaussian(keys[3], (SECTIONS, TOKENS, D), 0.5, 3.0, ((0, 16), (1, 16)))
    back_experts = draw_back_experts(jax.random.fold_in(keys[13], 71), 0)
    back_weight = jnp.clip(0.5 + 1.0 * jax.random.uniform(keys[5], (SECTIONS, TOKENS, TOPK), jnp.float32) ** block_levels(keys[5], (SECTIONS, TOKENS, TOPK), ((0, 16), (1, 16)), -0.2, 0.2), 0.5, 1.5).astype(jnp.bfloat16)
    back_cotangent = gaussian(keys[6], (SECTIONS, TOKENS, D), 1.0, 6.0, ((0, 16), (1, 16)))
    norm_gain = jnp.clip(1.0 + 0.18 * jax.random.normal(keys[7], (SECTIONS, D), jnp.float32), 0.099609375, 1.8984375).astype(jnp.bfloat16)
    w_gate = gaussian(keys[8], (SECTIONS, SHARDS, D, FF_DEV), D ** -0.5, 0.09375, ((0, 16), (1, 16)))
    w_up = gaussian(keys[9], (SECTIONS, SHARDS, D, FF_DEV), D ** -0.5, 0.09375, ((0, 16), (1, 16)))
    w_down = gaussian(keys[10], (SECTIONS, SHARDS, FF_DEV, D), FF ** -0.5, 0.1875, ((0, 16), (1, 16)))
    saved_gate = gaussian(keys[11], (SECTIONS, SHARDS, ROWS, FF_DEV), 1.0, 6.0, ((0, 16), (1, 16)))
    saved_up = gaussian(keys[12], (SECTIONS, SHARDS, ROWS, FF_DEV), 1.0, 6.0, ((0, 16), (1, 16)))
    return {"fwd_rows": fwd_rows, "fwd_experts": fwd_experts, "fwd_weight": fwd_weight, "back_rows": back_rows, "back_experts": back_experts, "back_weight": back_weight, "back_cotangent": back_cotangent, "norm_gain": norm_gain, "w_gate": w_gate, "w_up": w_up, "w_down": w_down, "saved_gate": saved_gate, "saved_up": saved_up}


epsilon = 1e-06

def normalize(rows_in, gain_wide):
    widened = rows_in.astype(jnp.float32)
    rscale = lax.rsqrt(lax.optimization_barrier(jnp.mean(widened * widened, axis=-1, keepdims=True)) + epsilon)
    unit_rows = widened * rscale
    return ((unit_rows * gain_wide).astype(jnp.bfloat16), unit_rows, rscale)

def transposed(left, right):
    return lax.dot_general(left, right, (((1,), (1,)), ((), ())), preferred_element_type=jnp.float32)

def route_tables(expert_ids):
    token_count = expert_ids.shape[0]
    block_count = token_count // TOK_DEV
    one_hot = (expert_ids[:, :, None] == jnp.arange(EXPERTS, dtype=jnp.int32)[None, None, :]).astype(jnp.int32)
    named = lax.optimization_barrier(jnp.sum(one_hot, axis=1, dtype=jnp.int32))
    by_block = named.reshape(block_count, TOK_DEV, EXPERTS)
    ranks = (jnp.cumsum(by_block, axis=1, dtype=jnp.int32) - by_block).reshape(token_count, EXPERTS)
    slot_of = lax.optimization_barrier(jnp.sum(one_hot * ranks[:, None, :], axis=2, dtype=jnp.int32))
    block_of = jnp.arange(token_count, dtype=jnp.int32) // TOK_DEV
    row_of = (block_of[:, None] * CAP + slot_of).astype(jnp.int32)
    positions = jnp.broadcast_to(jnp.arange(token_count, dtype=jnp.int32)[:, None], expert_ids.shape)
    token_of = jnp.zeros((EXPERTS, block_count * CAP), jnp.int32).at[expert_ids, row_of].set(positions)
    return (one_hot, row_of, token_of)

def section_pass(items):
    fwd_one, fwd_ids, fwd_gates, back_one, back_ids, back_gates, cot_one, gain_one, gate_all, up_all, down_all, saved_g, saved_u = items
    gain_wide = gain_one.astype(jnp.float32)
    normed_f = normalize(fwd_one, gain_wide)[0]
    fwd_hot, fwd_row, fwd_token = route_tables(fwd_ids)
    fwd_shard_tokens = jnp.repeat(fwd_token, HSPLIT, axis=0)

    def forward_shard(shard_items):
        gate_mat, up_mat, down_mat, token_list = shard_items
        picked = jnp.take(normed_f, token_list, axis=0)
        gate_f = jnp.dot(picked, gate_mat, preferred_element_type=jnp.float32)
        up_f = jnp.dot(picked, up_mat, preferred_element_type=jnp.float32)
        hidden_f = (jax.nn.silu(gate_f) * up_f).astype(jnp.bfloat16)
        return jnp.dot(hidden_f, down_mat, preferred_element_type=jnp.float32).astype(jnp.bfloat16)
    part_f = lax.map(forward_shard, (gate_all, up_all, down_all, fwd_shard_tokens))
    width = part_f.shape[-1]
    combined_f = lax.optimization_barrier(jnp.sum(part_f.astype(jnp.float32).reshape(EXPERTS, HSPLIT, -1, width), axis=1))
    picked_f = combined_f[fwd_ids, fwd_row]
    branch = lax.optimization_barrier(jnp.sum(fwd_gates.astype(jnp.float32)[:, :, None] * picked_f, axis=1))
    layer_out = (fwd_one.astype(jnp.float32) + branch).astype(jnp.bfloat16)
    back_hot, back_row, back_token = route_tables(back_ids)
    weight_table = lax.optimization_barrier(jnp.sum(back_gates.astype(jnp.float32)[:, :, None] * back_hot.astype(jnp.float32), axis=1))
    slot_weight = weight_table[back_token, jnp.arange(EXPERTS, dtype=jnp.int32)[:, None]]
    back_shard_tokens = jnp.repeat(back_token, HSPLIT, axis=0)
    back_shard_weight = jnp.repeat(slot_weight, HSPLIT, axis=0)

    def backward_shard(shard_items):
        gate_mat, up_mat, down_mat, token_list, weight_list, gate_pre, up_pre = shard_items
        cot_picked = jnp.take(cot_one, token_list, axis=0)
        d_hidden = weight_list[:, None] * transposed(cot_picked, down_mat)
        gate_b = gate_pre.astype(jnp.float32)
        up_b = up_pre.astype(jnp.float32)
        sigmoid_gate = jax.nn.sigmoid(gate_b)
        d_gate = (d_hidden * up_b * sigmoid_gate * (1.0 + gate_b * (1.0 - sigmoid_gate))).astype(jnp.bfloat16)
        d_up = (d_hidden * gate_b * sigmoid_gate).astype(jnp.bfloat16)
        return (transposed(d_gate, gate_mat) + transposed(d_up, up_mat)).astype(jnp.bfloat16)
    part_b = lax.map(backward_shard, (gate_all, up_all, down_all, back_shard_tokens, back_shard_weight, saved_g, saved_u))
    combined_b = lax.optimization_barrier(jnp.sum(part_b.astype(jnp.float32).reshape(EXPERTS, HSPLIT, -1, width), axis=1))
    d_normed = lax.optimization_barrier(jnp.sum(combined_b[back_ids, back_row], axis=1))
    unit_b, scale_b = normalize(back_one, gain_wide)[1:]
    d_unit = d_normed * gain_wide
    d_rows = scale_b * (d_unit - unit_b * lax.optimization_barrier(jnp.mean(d_unit * unit_b, axis=-1, keepdims=True)))
    grad_in = (cot_one.astype(jnp.float32) + d_rows).astype(jnp.bfloat16)
    return (layer_out, grad_in)

def reference(fwd_rows, fwd_experts, fwd_weight, back_rows, back_experts, back_weight, back_cotangent, norm_gain, w_gate, w_up, w_down, saved_gate, saved_up):
    outputs, grads = lax.map(section_pass, (fwd_rows, fwd_experts, fwd_weight, back_rows, back_experts, back_weight, back_cotangent, norm_gain, w_gate, w_up, w_down, saved_gate, saved_up))
    zero_section = jnp.zeros_like(outputs[:1])
    next_input = jnp.concatenate([zero_section, outputs[:-1]], axis=0)
    prev_grad = jnp.concatenate([grads[1:], zero_section], axis=0)
    return (next_input, prev_grad)
```

```python
import jax
import jax.numpy as jnp
from jax import lax
from jax.experimental import pallas as pl
from jax.experimental.pallas import tpu as pltpu
from jax.sharding import PartitionSpec as P

MESH = pl.DeviceIdType.MESH
D = 3584
FF = 256
TOK = 64
CAP = 32
HALF = 128
FULL = 256
COLS = 512
CHUNKS = D // COLS
EPS = 1e-06
F32 = jnp.float32
BF16 = jnp.bfloat16


def dot(left, right):
    return lax.dot_general(left, right, (((1,), (0,)), ((), ())), preferred_element_type=F32)


def dot_nt(left, right):
    return lax.dot_general(left, right, (((1,), (1,)), ((), ())), preferred_element_type=F32)


def rows(ref, slot, count=1):
    return ref.at[pl.ds(slot * CAP, count * CAP), :]


def selection(ids, slot_experts):
    lane = lax.broadcasted_iota(jnp.int32, (TOK, HALF), 1)
    slot = lax.shift_right_logical(lane, 5)
    rank_of = (lane & (CAP - 1)).astype(F32)
    expert = jnp.zeros((TOK, HALF), jnp.int32)
    for s, e in enumerate(slot_experts):
        expert = jnp.where(slot == s, e, expert)
    first = ids[:, 0:1] == expert
    second = ids[:, 1:2] == expert
    named = jnp.where(first | second, 1.0, 0.0)
    below = lax.broadcasted_iota(jnp.int32, (TOK, TOK), 1) < lax.broadcasted_iota(
        jnp.int32, (TOK, TOK), 0
    )
    ranks = dot(jnp.where(below, 1.0, 0.0).astype(BF16), named.astype(BF16))
    hit = ranks == rank_of
    return first & hit, second & hit


def weigh(masks, weights):
    first, second = masks
    return jnp.where(first, weights[:, 0:1], 0.0) + jnp.where(second, weights[:, 1:2], 0.0)


def kernel(
    fids, fw, bids, bw, gain, xf_h, xb_h, ct_h, wg_h, wu_h, wd_h, sg_h, su_h,
    nxt, prv,
    xf, xb, ct, wg, wu, wd, wdo, sg, su,
    csend, fsend, crow, frow,
    dho, dsend, drecv, dg, du,
    bsend, brecv, bown, zsb, zrb, zdb, retb,
    hown, hsend, hrecv, zsf, zrf, zdf, retf,
    fout, gout, dn,
    ld, s_wd, r_wd, s_c, r_c, s_f, r_f, s_fy, r_fy, s_d, r_d, s_by, r_by,
    s_bp, r_bp, s_bd, r_bd, s_h, r_h, s_fp, r_fp, s_fd, r_fd, s_out, r_out,
):
    p = lax.axis_index("pipe")
    me = lax.axis_index("expert")
    z = lax.div(me, 2)
    y = lax.rem(me, 2)
    dz = 2 * lax.rem(z, 2) - 1

    def at_z(zz):
        return lax.rem(zz + 8, 8)

    def dev(zz):
        return (p, at_z(zz) * 2 + y)

    targets = [z, z + dz, z - 2 * dz, z + 3 * dz]
    sources = [z, z + dz, z + 2 * dz, z + 3 * dz]
    pz = z - dz
    partner = dev(pz)
    y_partner = (p, z * 2 + 1 - y)
    slot_experts = [lax.div(at_z(t), 2) for t in targets]
    block_z = [at_z(s) for s in sources] + [at_z(pz - k * dz) for k in range(4)]

    barrier = pltpu.get_barrier_semaphore()
    friends = [
        partner,
        dev(z + dz),
        dev(z + 2 * dz),
        dev(z - 2 * dz),
        dev(z + 3 * dz),
        y_partner,
        (lax.rem(p + 1, 16), me),
        (lax.rem(p + 15, 16), me),
    ]
    for friend in friends:
        pl.semaphore_signal(barrier, inc=1, device_id=friend, device_id_type=MESH)

    loads = {}
    for i, (name, src, dst) in enumerate(
        [
            ("ct", ct_h, ct),
            ("xf", xf_h, xf),
            ("wd", wd_h, wd),
            ("wg", wg_h, wg),
            ("wu", wu_h, wu),
            ("sg", sg_h, sg),
            ("su", su_h, su),
            ("xb", xb_h, xb),
        ]
    ):
        loads[name] = pltpu.make_async_copy(src, dst, ld.at[i])
        loads[name].start()

    sent = []

    def remote(src, dst, s_sem, r_sem, target):
        return pltpu.make_async_remote_copy(
            src_ref=src, dst_ref=dst, send_sem=s_sem, recv_sem=r_sem,
            device_id=target, device_id_type=MESH,
        )

    def send(cp):
        cp.start()
        sent.append(cp)

    bmask = selection(bids[...], slot_experts)
    b_hot = weigh(bmask, jnp.ones((TOK, 2), F32)).astype(BF16)
    b_gather = weigh(bmask, bw[...].astype(F32)).T.astype(BF16)
    loads["ct"].wait()
    for c in range(CHUNKS):
        cs = slice(c * COLS, (c + 1) * COLS)
        csend[:, cs] = dot(b_gather, ct[:, cs]).astype(BF16)
    crow[0:CAP, :] = csend[0:CAP, :]

    pl.semaphore_wait(barrier, len(friends))

    wd_copies = [
        remote(wd_h.at[pl.ds(i * 64, 64), :], wdo.at[pl.ds(i * 64, 64), :], s_wd.at[i], r_wd.at[i], y_partner)
        for i in range(4)
    ]
    for cp in wd_copies:
        send(cp)

    def z_copies(block, out, s_sem, r_sem):
        cps = [None]
        for k in (1, 2, 3):
            cps.append(remote(rows(block, k), rows(out, k), s_sem.at[k], r_sem.at[k], dev(targets[k])))
        for k in range(4):
            cps.append(remote(rows(out, k), rows(out, 4 + k), s_sem.at[4 + k], r_sem.at[4 + k], partner))
        return cps

    c_cp = z_copies(csend, crow, s_c, r_c)
    for k in (3, 2, 1, 4):
        send(c_cp[k])

    fmask = selection(fids[...], slot_experts)
    f_hot = weigh(fmask, jnp.ones((TOK, 2), F32)).T.astype(BF16)
    f_weights = weigh(fmask, fw[...].astype(F32)).astype(BF16)
    gain_wide = gain[...].astype(F32)
    loads["xf"].wait()
    wide = xf[...].astype(F32)
    scale = lax.rsqrt(jnp.mean(wide * wide, axis=-1, keepdims=True) + EPS)
    fout[...] = (wide * scale * gain_wide).astype(BF16)
    for c in range(CHUNKS):
        cs = slice(c * COLS, (c + 1) * COLS)
        fsend[:, cs] = dot(f_hot, fout[:, cs]).astype(BF16)
    frow[0:CAP, :] = fsend[0:CAP, :]

    f_cp = z_copies(fsend, frow, s_f, r_f)
    fy_cp = [
        remote(rows(frow, j), rows(frow, 8 + j), s_fy.at[j], r_fy.at[j], y_partner) for j in range(8)
    ]

    for k in (1, 2, 3):
        c_cp[k].wait_recv()
        send(c_cp[4 + k])
    for k in (3, 2, 1, 4):
        send(f_cp[k])

    loads["wd"].wait()
    dho[0:HALF, :] = dot_nt(crow[0:HALF, :], wd[...])
    for k in range(4):
        c_cp[4 + k].wait_recv()
    dho[HALF:FULL, :] = dot_nt(crow[HALF:FULL, :], wd[...])

    send(fy_cp[0])
    f_cp[1].wait_recv()
    send(f_cp[5])
    send(fy_cp[1])

    for cp in wd_copies:
        cp.wait_recv()
    dsend[...] = dot_nt(crow[...], wdo[...]).astype(BF16)
    d_cp = remote(dsend, drecv, s_d.at[0], r_d.at[0], y_partner)
    send(d_cp)

    for k in (2, 3):
        f_cp[k].wait_recv()
        send(f_cp[4 + k])
        send(fy_cp[k])

    loads["sg"].wait()
    loads["su"].wait()

    def activation_grad(j, column, d_hidden):
        start = pl.multiple_of((block_z[j] * 2 + column) * CAP, CAP)
        gate_b = sg[pl.ds(start, CAP), :].astype(F32)
        up_b = su[pl.ds(start, CAP), :].astype(F32)
        sigmoid = jax.nn.sigmoid(gate_b)
        d_gate = d_hidden * up_b * sigmoid * (1.0 + gate_b * (1.0 - sigmoid))
        d_up = d_hidden * gate_b * sigmoid
        return d_gate.astype(BF16), d_up.astype(BF16)

    for j in range(8):
        js = slice(j * CAP, (j + 1) * CAP)
        d_gate, d_up = activation_grad(j, y, dho[js, :])
        dg[js, :] = d_gate
        du[js, :] = d_up
    d_cp.wait_recv()
    for j in range(8):
        js = slice(j * CAP, (j + 1) * CAP)
        ks = slice(FULL + j * CAP, FULL + (j + 1) * CAP)
        d_gate, d_up = activation_grad(j, 1 - y, drecv[js, :].astype(F32))
        dg[ks, :] = d_gate
        du[ks, :] = d_up

    loads["wg"].wait()
    loads["wu"].wait()
    by_cp = [remote(rows(bsend, j), rows(brecv, j), s_by.at[j], r_by.at[j], y_partner) for j in range(8)]
    for c in range(CHUNKS):
        cs = slice(c * COLS, (c + 1) * COLS)
        bsend[:, cs] = (
            dot_nt(dg[FULL : 2 * FULL, :], wg[cs, :]) + dot_nt(du[FULL : 2 * FULL, :], wu[cs, :])
        ).astype(BF16)
    for k in range(4):
        send(by_cp[4 + k])
        send(by_cp[k])
    for c in range(CHUNKS):
        cs = slice(c * COLS, (c + 1) * COLS)
        bown[:, cs] = dot_nt(dg[0:FULL, :], wg[cs, :]) + dot_nt(du[0:FULL, :], wu[cs, :])

    def hidden(block):
        gate = dot(block, wg[...])
        up = dot(block, wu[...])
        return (gate * jax.nn.sigmoid(gate) * up).astype(BF16)

    for k in range(4):
        f_cp[4 + k].wait_recv()
    hown[...] = hidden(frow[0:FULL, :])

    h_cp = [
        remote(rows(hsend, 4 * g, 4), rows(hrecv, 4 * g, 4), s_h.at[g], r_h.at[g], y_partner) for g in range(2)
    ]

    def partner_hidden(g):
        for j in range(4 * g, 4 * g + 4):
            fy_cp[j].wait_recv()
        hsend[g * HALF : (g + 1) * HALF, :] = hidden(frow[FULL + g * HALF : FULL + (g + 1) * HALF, :])
        send(h_cp[g])

    partner_hidden(0)

    bp_cp = [remote(rows(zsb, k), rows(zrb, k), s_bp.at[k], r_bp.at[k], partner) for k in range(4)]
    bd_cp = [None] + [
        remote(rows(zdb, k), rows(retb, k), s_bd.at[k], r_bd.at[k], dev(sources[k])) for k in (1, 2, 3)
    ]
    for k in range(4):
        ks = slice(k * CAP, (k + 1) * CAP)
        js = slice(HALF + k * CAP, HALF + (k + 1) * CAP)
        by_cp[4 + k].wait_recv()
        zsb[ks, :] = (bown[js, :] + brecv[js, :].astype(F32)).astype(BF16)
        send(bp_cp[k])
        if k == 1:
            for m in range(4):
                send(fy_cp[4 + m])
    for k in (3, 2, 1, 0):
        ks = slice(k * CAP, (k + 1) * CAP)
        by_cp[k].wait_recv()
        bp_cp[k].wait_recv()
        total = (bown[ks, :] + brecv[ks, :].astype(F32) + zrb[ks, :].astype(F32)).astype(BF16)
        if k == 0:
            retb[ks, :] = total
        else:
            zdb[ks, :] = total
            send(bd_cp[k])

    fp_cp = [remote(rows(zsf, k), rows(zrf, k), s_fp.at[k], r_fp.at[k], partner) for k in range(4)]
    fd_cp = [None] + [
        remote(rows(zdf, k), rows(retf, k), s_fd.at[k], r_fd.at[k], dev(sources[k])) for k in (1, 2, 3)
    ]
    partner_hidden(1)
    h_cp[1].wait_recv()
    for c in range(CHUNKS):
        cs = slice(c * COLS, (c + 1) * COLS)
        zsf[:, cs] = (
            dot(hown[HALF:FULL, :], wd[:, cs]) + dot(hrecv[HALF:FULL, :], wdo[:, cs])
        ).astype(BF16)
    for k in (3, 2, 1, 0):
        send(fp_cp[k])

    for k in (1, 2, 3):
        bd_cp[k].wait_recv()
    loads["xb"].wait()
    wide_b = xb[...].astype(F32)
    scale_b = lax.rsqrt(jnp.mean(wide_b * wide_b, axis=-1, keepdims=True) + EPS)
    inner = jnp.zeros((TOK, 1), F32)
    for c in range(CHUNKS):
        cs = slice(c * COLS, (c + 1) * COLS)
        part = dot(b_hot, retb[:, cs]) * gain_wide[:, cs]
        dn[:, cs] = part
        inner = inner + jnp.sum(part * (xb[:, cs].astype(F32) * scale_b), axis=-1, keepdims=True)
    inner = inner * (1.0 / D)
    for c in range(CHUNKS):
        cs = slice(c * COLS, (c + 1) * COLS)
        unit = xb[:, cs].astype(F32) * scale_b
        gout[:, cs] = (ct[:, cs].astype(F32) + scale_b * (dn[:, cs] - unit * inner)).astype(BF16)
    b_out = remote(gout, prv, s_out.at[1], r_out.at[1], (lax.rem(p + 15, 16), me))

    @pl.when(p > 0)
    def _():
        b_out.start()

    h_cp[0].wait_recv()
    for c in range(CHUNKS):
        cs = slice(c * COLS, (c + 1) * COLS)
        bown[0:HALF, cs] = dot(hown[0:HALF, :], wd[:, cs]) + dot(hrecv[0:HALF, :], wdo[:, cs])
    for k in (3, 2, 1, 0):
        ks = slice(k * CAP, (k + 1) * CAP)
        fp_cp[k].wait_recv()
        total = (bown[ks, :] + zrf[ks, :].astype(F32)).astype(BF16)
        if k == 0:
            retf[ks, :] = total
        else:
            zdf[ks, :] = total
            send(fd_cp[k])
    for k in (1, 2, 3):
        fd_cp[k].wait_recv()
    for c in range(CHUNKS):
        cs = slice(c * COLS, (c + 1) * COLS)
        fout[:, cs] = (xf[:, cs].astype(F32) + dot(f_weights, retf[:, cs])).astype(BF16)
    f_out = remote(fout, nxt, s_out.at[0], r_out.at[0], (lax.rem(p + 1, 16), me))

    @pl.when(p < 15)
    def _():
        f_out.start()

    @pl.when(p == 0)
    def _():
        gout[...] = jnp.zeros_like(gout)
        zero = pltpu.make_async_copy(gout, nxt, ld.at[8])
        zero.start()
        zero.wait()

    @pl.when(p == 15)
    def _():
        fout[...] = jnp.zeros_like(fout)
        zero = pltpu.make_async_copy(fout, prv, ld.at[9])
        zero.start()
        zero.wait()

    for cp in sent:
        cp.wait_send()

    @pl.when(p > 0)
    def _():
        f_out.wait_recv()
        b_out.wait_send()

    @pl.when(p < 15)
    def _():
        b_out.wait_recv()
        f_out.wait_send()


def body(
    fwd_rows,
    fwd_experts,
    fwd_weight,
    back_rows,
    back_experts,
    back_weight,
    back_cotangent,
    norm_gain,
    w_gate,
    w_up,
    w_down,
    saved_gate,
    saved_up,
):
    vmem = pl.BlockSpec(memory_space=pltpu.VMEM)
    hbm = pl.BlockSpec(memory_space=pl.ANY)
    dma = pltpu.SemaphoreType.DMA

    def wide(count, kind=BF16):
        return pltpu.VMEM((count, D), kind)

    def narrow(count, kind=BF16):
        return pltpu.VMEM((count, FF), kind)

    outs = pl.pallas_call(
        kernel,
        out_shape=(jax.ShapeDtypeStruct((TOK, D), BF16), jax.ShapeDtypeStruct((TOK, D), BF16)),
        in_specs=[vmem] * 5 + [hbm] * 8,
        out_specs=(hbm, hbm),
        scratch_shapes=[
            wide(TOK), wide(TOK), wide(TOK),
            narrow(D), narrow(D), wide(FF), wide(FF), narrow(512), narrow(512),
            wide(HALF), wide(HALF), wide(FULL), wide(2 * FULL),
            narrow(FULL, F32), narrow(FULL), narrow(FULL), narrow(512), narrow(512),
            wide(FULL), wide(FULL), wide(FULL, F32), wide(HALF), wide(HALF), wide(HALF), wide(HALF),
            narrow(FULL), narrow(FULL), narrow(FULL), wide(HALF), wide(HALF), wide(HALF), wide(HALF),
            wide(TOK), wide(TOK), wide(TOK, F32),
            dma((10,)), dma((4,)), dma((4,)), dma((8,)), dma((8,)), dma((8,)), dma((8,)),
            dma((8,)), dma((8,)), dma((1,)), dma((1,)), dma((8,)), dma((8,)),
            dma((4,)), dma((4,)), dma((4,)), dma((4,)), dma((2,)), dma((2,)),
            dma((4,)), dma((4,)), dma((4,)), dma((4,)), dma((2,)), dma((2,)),
        ],
        compiler_params=pltpu.CompilerParams(
            collective_id=0, has_side_effects=True, vmem_limit_bytes=56 * 2**20
        ),
        cost_estimate=pl.CostEstimate(flops=5_700_000_000, bytes_accessed=10_000_000, transcendentals=400_000),
    )(
        fwd_experts[0],
        fwd_weight[0],
        back_experts[0],
        back_weight[0],
        norm_gain,
        fwd_rows[0],
        back_rows[0],
        back_cotangent[0],
        w_gate[0, 0],
        w_up[0, 0],
        w_down[0, 0],
        saved_gate[0, 0],
        saved_up[0, 0],
    )
    return outs[0][None], outs[1][None]


def solution(mesh):
    rows3 = P("pipe", "expert", None)
    rows4 = P("pipe", "expert", None, None)
    placed = (rows3,) * 7 + (P("pipe", None),) + (rows4,) * 5
    return jax.shard_map(
        body,
        mesh=mesh,
        in_specs=placed,
        out_specs=(rows3, rows3),
        check_vma=False,
    )
```

```python
import jax
import jax.numpy as jnp
from jax import lax
from jax.experimental import pallas as pl
from jax.experimental.pallas import tpu as pltpu
from jax.sharding import PartitionSpec as P

MESH = pl.DeviceIdType.MESH
D = 3584
FF = 256
TOK = 64
CAP = 32
HALF = 128
FULL = 256
COLS = 512
CHUNKS = [slice(c, c + COLS) for c in range(0, D, COLS)]
W_PARTS = 8
EPS = 1e-06
F32 = jnp.float32
BF16 = jnp.bfloat16

ORDER = [
    "~prepC", "+C4", "+C1", "+W0", "+W1", "+W2", "+W3", "~prepF", "+F2", "+F3", "+W4", "+W5", "?C1",
    "+W6", "+F4", "+W7", "?F3", "+Y3", "?F2", "+F6", "+F7", "+C2", "+F1", "?W0", "?F1", "+F5",
    "?F6", "+Y6", "+C3", "?W1", "?W2", "?F7", "?W3", "?C2", "+Y2", "+C6", "?W4", "?F4", "+Y7",
    "+C5", "?W5", "?W6", "?Y6", "?C3", "+C7", "?F5", "?Y3", "?Y2", "~h2", "+H2", "+Y1", "?C5",
    "?Y7", "~h3", "+H3", "~hown", "?W7", "+Y5", "?H2", "~fo2", "+FP2", "?C6", "?H3", "~fo3", "+FP3",
    "+Y0", "?FP2", "~fa2", "+FD2", "?C7", "?C4", "?Y1", "?Y5", "~h1", "+H1", "~dhoth", "+D", "?FP3",
    "~fa3", "+FD3", "+Y4", "?H1", "~fo1", "?Y0", "+FP1", "?D", "~bs", "+G7", "~dhown", "~actown",
    "?Y4", "~h0", "+H0", "+G5", "+G3", "~bown", "+G6", "?G7", "~ba3", "+G4", "+BP3", "?FD2", "?H0",
    "~fo0", "+FP0", "?G5", "~ba1", "?FP1", "?BP3", "+BP1", "~fa1", "?G3", "+FD1", "?FP0", "+G1",
    "~bb3", "+BD3", "?G6", "?FD3", "~ba2", "+G2", "+BP2", "?G4", "?BP1", "~ba0", "+BP0", "?G1",
    "~bb1", "+G0", "+BD1", "?G2", "?BP2", "~bb2", "+BD2", "?BD3", "?FD1", "?BP0", "~fa0", "~cf",
    "+RF", "?G0", "~bb0", "?BD1", "?BD2", "~cb", "+RB", "?RF", "?RB"
]


def dot(left, right):
    return lax.dot_general(left, right, (((1,), (0,)), ((), ())), preferred_element_type=F32)


def dot_nt(left, right):
    return lax.dot_general(left, right, (((1,), (1,)), ((), ())), preferred_element_type=F32)


def place(slot):
    return 2 * (slot % 4) + slot // 4


def span(position, count=1, base=0):
    return slice(base + position * CAP, base + (position + count) * CAP)


def rows(ref, position, count=1):
    return ref.at[pl.ds(position * CAP, count * CAP), :]


def selection(ids, slot_experts):
    line = lax.broadcasted_iota(jnp.int32, (HALF, TOK), 0)
    slot = lax.shift_right_logical(line, 5)
    rank_of = (line & (CAP - 1)).astype(F32)
    expert = jnp.zeros((HALF, TOK), jnp.int32)
    for s, e in enumerate(slot_experts):
        expert = jnp.where(slot == s, e, expert)
    first = ids[0:1, :] == expert
    second = ids[1:2, :] == expert
    named = jnp.where(first | second, 1.0, 0.0)
    before = lax.broadcasted_iota(jnp.int32, (TOK, TOK), 0) < lax.broadcasted_iota(
        jnp.int32, (TOK, TOK), 1
    )
    ranks = dot(named.astype(BF16), jnp.where(before, 1.0, 0.0).astype(BF16))
    hit = ranks == rank_of
    return first & hit, second & hit


def weigh(masks, weights):
    first, second = masks
    return jnp.where(first, weights[0:1, :], 0.0) + jnp.where(second, weights[1:2, :], 0.0)


def kernel(
    fids, fw, bids, bw, gain, xf_h, xb_h, ct_h, wg_h, wu_h, wd_h, sg_h, su_h,
    nxt, prv,
    xf, xb, ct, wg, wu, wd, wdo, sg, su,
    csend, fsend, crow, frow,
    dho, dsend, drecv, dg, du,
    bsend, brecv, bown, zsb, zrb, zdb, retb,
    hown, hsend, hrecv, fown, zsf, zrf, zdf, retf,
    fout, gout, dn, b_hot, f_hot,
    ld, s_w, r_w, s_c, r_c, s_f, r_f, s_y, r_y, s_d, r_d, s_g, r_g,
    s_bp, r_bp, s_bd, r_bd, s_h, r_h, s_fp, r_fp, s_fd, r_fd, s_out, r_out,
):
    p = lax.axis_index("pipe")
    me = lax.axis_index("expert")
    z = lax.div(me, 2)
    y = lax.rem(me, 2)
    dz = 2 * lax.rem(z, 2) - 1

    def at_z(zz):
        return lax.rem(zz + 8, 8)

    def dev(zz):
        return (p, at_z(zz) * 2 + y)

    targets = [z, z + dz, z - 2 * dz, z + 3 * dz]
    sources = [z, z + dz, z + 2 * dz, z + 3 * dz]
    pz = z - dz
    z_partner = dev(pz)
    y_partner = (p, z * 2 + 1 - y)
    later = (lax.rem(p + 1, 16), me)
    earlier = (lax.rem(p + 15, 16), me)
    slot_experts = [lax.div(at_z(t), 2) for t in targets]
    block_z = [at_z(s) for s in sources] + [at_z(pz - k * dz) for k in range(4)]

    barrier = pltpu.get_barrier_semaphore()
    friends = [
        z_partner,
        dev(z + dz),
        dev(z + 2 * dz),
        dev(z - 2 * dz),
        dev(z + 3 * dz),
        y_partner,
        later,
        earlier,
    ]
    for friend in friends:
        pl.semaphore_signal(barrier, inc=1, device_id=friend, device_id_type=MESH)

    loads = {}
    for i, (name, src, dst) in enumerate(
        [
            ("ct", ct_h, ct),
            ("xf", xf_h, xf),
            ("wd", wd_h, wd),
            ("wg", wg_h, wg),
            ("wu", wu_h, wu),
            ("sg", sg_h, sg),
            ("su", su_h, su),
            ("xb", xb_h, xb),
        ]
    ):
        loads[name] = pltpu.make_async_copy(src, dst, ld.at[i])
        loads[name].start()

    def need(*names):
        for name in names:
            if name in loads:
                loads.pop(name).wait()

    copies = {}

    def remote(name, src, dst, s_sem, r_sem, target):
        copies[name] = pltpu.make_async_remote_copy(
            src_ref=src, dst_ref=dst, send_sem=s_sem, recv_sem=r_sem,
            device_id=target, device_id_type=MESH,
        )

    part = FF // W_PARTS
    for i in range(W_PARTS):
        cut = pl.ds(i * part, part)
        remote(f"W{i}", wd_h.at[cut, :], wdo.at[cut, :], s_w.at[i], r_w.at[i], y_partner)
    for name, block, out, s_sem, r_sem in (("C", csend, crow, s_c, r_c), ("F", fsend, frow, s_f, r_f)):
        for k in (1, 2, 3):
            remote(
                f"{name}{k}", rows(block, k), rows(out, place(k)), s_sem.at[k], r_sem.at[k], dev(targets[k])
            )
        for k in range(4):
            remote(
                f"{name}{4 + k}", rows(out, place(k)), rows(out, place(4 + k)),
                s_sem.at[4 + k], r_sem.at[4 + k], z_partner,
            )
    for j in range(8):
        remote(f"Y{j}", rows(frow, place(j)), rows(frow, 8 + place(j)), s_y.at[j], r_y.at[j], y_partner)
        remote(f"G{j}", rows(bsend, place(j)), rows(brecv, place(j)), s_g.at[j], r_g.at[j], y_partner)
    remote("D", dsend, drecv, s_d.at[0], r_d.at[0], y_partner)
    for k in range(4):
        remote(f"H{k}", rows(hsend, 2 * k, 2), rows(hrecv, 2 * k, 2), s_h.at[k], r_h.at[k], y_partner)
        remote(f"BP{k}", rows(zsb, k), rows(zrb, k), s_bp.at[k], r_bp.at[k], z_partner)
        remote(f"FP{k}", rows(zsf, k), rows(zrf, k), s_fp.at[k], r_fp.at[k], z_partner)
    for k in (1, 2, 3):
        remote(f"BD{k}", rows(zdb, k), rows(retb, k), s_bd.at[k], r_bd.at[k], dev(sources[k]))
        remote(f"FD{k}", rows(zdf, k), rows(retf, k), s_fd.at[k], r_fd.at[k], dev(sources[k]))
    remote("RF", fout, nxt, s_out.at[0], r_out.at[0], later)
    remote("RB", gout, prv, s_out.at[1], r_out.at[1], earlier)

    computed = {}

    def compute(name, function, *given):
        computed[name] = (function, given)

    def cotangent_blocks():
        masks = selection(bids[...], slot_experts)
        b_hot[...] = weigh(masks, jnp.ones((2, TOK), F32)).T.astype(BF16)
        gather = weigh(masks, bw[...].astype(F32)).astype(BF16)
        need("ct")
        for cs in CHUNKS:
            csend[:, cs] = dot(gather, ct[:, cs]).astype(BF16)
        crow[span(0), :] = csend[span(0), :]
        pl.semaphore_wait(barrier, len(friends))

    def forward_blocks():
        masks = selection(fids[...], slot_experts)
        gather = weigh(masks, jnp.ones((2, TOK), F32)).astype(BF16)
        f_hot[...] = weigh(masks, fw[...].astype(F32)).T.astype(BF16)
        need("xf")
        wide = xf[...].astype(F32)
        scale = lax.rsqrt(jnp.mean(wide * wide, axis=-1, keepdims=True) + EPS)
        fout[...] = (wide * scale * gain[...].astype(F32)).astype(BF16)
        for cs in CHUNKS:
            fsend[:, cs] = dot(gather, fout[:, cs]).astype(BF16)
        frow[span(0), :] = fsend[span(0), :]

    def own_d_hidden():
        need("wd")
        dho[...] = dot_nt(crow[...], wd[...])

    def other_d_hidden():
        dsend[...] = dot_nt(crow[...], wdo[...]).astype(BF16)

    def activation_grad(j, column, d_hidden):
        need("sg", "su")
        start = pl.multiple_of((block_z[j] * 2 + column) * CAP, CAP)
        gate_b = sg[pl.ds(start, CAP), :].astype(F32)
        up_b = su[pl.ds(start, CAP), :].astype(F32)
        sigmoid = jax.nn.sigmoid(gate_b)
        d_gate = d_hidden * up_b * sigmoid * (1.0 + gate_b * (1.0 - sigmoid))
        d_up = d_hidden * gate_b * sigmoid
        return d_gate.astype(BF16), d_up.astype(BF16)

    def own_activation():
        for j in range(8):
            js = span(place(j))
            dg[js, :], du[js, :] = activation_grad(j, y, dho[js, :])

    def other_gradient():
        need("wg", "wu")
        for j in range(8):
            js = span(place(j))
            ks = span(place(j), 1, FULL)
            dg[ks, :], du[ks, :] = activation_grad(j, 1 - y, drecv[js, :].astype(F32))
        for cs in CHUNKS:
            total = dot_nt(dg[FULL:, :], wg[cs, :]) + dot_nt(du[FULL:, :], wu[cs, :])
            bsend[:, cs] = total.astype(BF16)

    def own_gradient():
        need("wg", "wu")
        for cs in CHUNKS:
            bown[:, cs] = dot_nt(dg[0:FULL, :], wg[cs, :]) + dot_nt(du[0:FULL, :], wu[cs, :])

    def hidden(block):
        need("wg", "wu")
        gate = dot(block, wg[...])
        up = dot(block, wu[...])
        return (gate * jax.nn.sigmoid(gate) * up).astype(BF16)

    def own_hidden():
        hown[...] = hidden(frow[0:FULL, :])

    def other_hidden(k):
        hsend[span(2 * k, 2), :] = hidden(frow[span(2 * k, 2, FULL), :])

    def forward_partial(k):
        need("wd")
        ks = span(2 * k, 2)
        for cs in CHUNKS:
            total = dot(hown[ks, :], wd[:, cs]) + dot(hrecv[ks, :], wdo[:, cs])
            fown[span(k), cs] = total[0:CAP, :]
            zsf[span(k), cs] = total[CAP:, :].astype(BF16)

    def forward_sum(k):
        total = (fown[span(k), :] + zrf[span(k), :].astype(F32)).astype(BF16)
        out = zdf if k else retf
        out[span(k), :] = total

    def gradient_partial(k):
        js = span(place(4 + k))
        zsb[span(k), :] = (bown[js, :] + brecv[js, :].astype(F32)).astype(BF16)

    def gradient_sum(k):
        js = span(place(k))
        total = bown[js, :] + brecv[js, :].astype(F32) + zrb[span(k), :].astype(F32)
        out = zdb if k else retb
        out[span(k), :] = total.astype(BF16)

    def forward_out():
        for cs in CHUNKS:
            fout[:, cs] = (xf[:, cs].astype(F32) + dot(f_hot[...], retf[:, cs])).astype(BF16)

    def gradient_out():
        need("xb")
        wide_b = xb[...].astype(F32)
        scale_b = lax.rsqrt(jnp.mean(wide_b * wide_b, axis=-1, keepdims=True) + EPS)
        gain_wide = gain[...].astype(F32)
        inner = jnp.zeros((TOK, 1), F32)
        for cs in CHUNKS:
            d_unit = dot(b_hot[...], retb[:, cs]) * gain_wide[:, cs]
            dn[:, cs] = d_unit
            inner = inner + jnp.sum(d_unit * (xb[:, cs].astype(F32) * scale_b), axis=-1, keepdims=True)
        inner = inner * (1.0 / D)
        for cs in CHUNKS:
            unit = xb[:, cs].astype(F32) * scale_b
            gout[:, cs] = (ct[:, cs].astype(F32) + scale_b * (dn[:, cs] - unit * inner)).astype(BF16)

    compute("prepC", cotangent_blocks)
    compute("prepF", forward_blocks)
    compute("dhown", own_d_hidden)
    compute("dhoth", other_d_hidden)
    compute("actown", own_activation)
    compute("bs", other_gradient)
    compute("bown", own_gradient)
    compute("hown", own_hidden)
    compute("cf", forward_out)
    compute("cb", gradient_out)
    for k in range(4):
        compute(f"h{k}", other_hidden, k)
        compute(f"fo{k}", forward_partial, k)
        compute(f"fa{k}", forward_sum, k)
        compute(f"ba{k}", gradient_partial, k)
        compute(f"bb{k}", gradient_sum, k)

    sent = []
    for step in ORDER:
        kind, name = step[0], step[1:]
        if kind == "~":
            function, given = computed[name]
            function(*given)
        elif name == "RF":
            if kind == "+":
                pl.when(p < 15)(copies[name].start)
            else:
                pl.when(p > 0)(copies[name].wait_recv)
        elif name == "RB":
            if kind == "+":
                pl.when(p > 0)(copies[name].start)
            else:
                pl.when(p < 15)(copies[name].wait_recv)
        elif kind == "+":
            copies[name].start()
            sent.append(name)
        else:
            copies[name].wait_recv()

    @pl.when(p == 0)
    def _():
        gout[...] = jnp.zeros_like(gout)
        zero = pltpu.make_async_copy(gout, nxt, ld.at[8])
        zero.start()
        zero.wait()

    @pl.when(p == 15)
    def _():
        fout[...] = jnp.zeros_like(fout)
        zero = pltpu.make_async_copy(fout, prv, ld.at[9])
        zero.start()
        zero.wait()

    for name in sent:
        copies[name].wait_send()
    pl.when(p < 15)(copies["RF"].wait_send)
    pl.when(p > 0)(copies["RB"].wait_send)


def hand_over(first, second, first_out, second_out, held, in_sem, out_sem):
    cut = TOK // 2
    steps = []
    for i, (src, dst) in enumerate(((first, first_out), (second, second_out))):
        for j in range(2):
            here = pl.ds(j * cut, cut)
            steps.append(
                (
                    pltpu.make_async_copy(src.at[here, :], held.at[i, here, :], in_sem.at[i, j]),
                    pltpu.make_async_copy(held.at[i, here, :], dst.at[here, :], out_sem.at[i, j]),
                )
            )
    for arrive, _ in steps:
        arrive.start()
    for arrive, leave in steps:
        arrive.wait()
        leave.start()
    for _, leave in steps:
        leave.wait()


def body(
    fwd_rows,
    fwd_experts,
    fwd_weight,
    back_rows,
    back_experts,
    back_weight,
    back_cotangent,
    norm_gain,
    w_gate,
    w_up,
    w_down,
    saved_gate,
    saved_up,
):
    vmem = pl.BlockSpec(memory_space=pltpu.VMEM)
    hbm = pl.BlockSpec(memory_space=pl.ANY)
    dma = pltpu.SemaphoreType.DMA
    out_shape = (jax.ShapeDtypeStruct((TOK, D), BF16), jax.ShapeDtypeStruct((TOK, D), BF16))

    def wide(count, kind=BF16):
        return pltpu.VMEM((count, D), kind)

    def narrow(count, kind=BF16):
        return pltpu.VMEM((count, FF), kind)

    outs = pl.pallas_call(
        kernel,
        out_shape=out_shape,
        in_specs=[vmem] * 5 + [hbm] * 8,
        out_specs=(hbm, hbm),
        scratch_shapes=[
            wide(TOK), wide(TOK), wide(TOK),
            narrow(D), narrow(D), wide(FF), wide(FF), narrow(512), narrow(512),
            wide(HALF), wide(HALF), wide(FULL), wide(2 * FULL),
            narrow(FULL, F32), narrow(FULL), narrow(FULL), narrow(512), narrow(512),
            wide(FULL), wide(FULL), wide(FULL, F32), wide(HALF), wide(HALF), wide(HALF), wide(HALF),
            narrow(FULL), narrow(FULL), narrow(FULL), wide(HALF, F32), wide(HALF), wide(HALF), wide(HALF),
            wide(HALF),
            wide(TOK), wide(TOK), wide(TOK, F32),
            pltpu.VMEM((TOK, HALF), BF16), pltpu.VMEM((TOK, HALF), BF16),
            dma((10,)), dma((W_PARTS,)), dma((W_PARTS,)), dma((8,)), dma((8,)), dma((8,)), dma((8,)),
            dma((8,)), dma((8,)), dma((1,)), dma((1,)), dma((8,)), dma((8,)),
            dma((4,)), dma((4,)), dma((4,)), dma((4,)), dma((4,)), dma((4,)),
            dma((4,)), dma((4,)), dma((4,)), dma((4,)), dma((2,)), dma((2,)),
        ],
        compiler_params=pltpu.CompilerParams(
            collective_id=0, has_side_effects=True, vmem_limit_bytes=56 * 2**20
        ),
        cost_estimate=pl.CostEstimate(flops=5_700_000_000, bytes_accessed=10_000_000, transcendentals=400_000),
    )(
        fwd_experts[0].T,
        fwd_weight[0].T,
        back_experts[0].T,
        back_weight[0].T,
        norm_gain,
        fwd_rows[0],
        back_rows[0],
        back_cotangent[0],
        w_gate[0, 0],
        w_up[0, 0],
        w_down[0, 0],
        saved_gate[0, 0],
        saved_up[0, 0],
    )
    outs = pl.pallas_call(
        hand_over,
        out_shape=out_shape,
        in_specs=[hbm, hbm],
        out_specs=(hbm, hbm),
        scratch_shapes=[pltpu.VMEM((2, TOK, D), BF16), dma((2, 2)), dma((2, 2))],
        compiler_params=pltpu.CompilerParams(vmem_limit_bytes=56 * 2**20),
    )(*outs)
    return outs[0][None], outs[1][None]


def solution(mesh):
    rows3 = P("pipe", "expert", None)
    rows4 = P("pipe", "expert", None, None)
    placed = (rows3,) * 7 + (P("pipe", None),) + (rows4,) * 5
    return jax.shard_map(
        body,
        mesh=mesh,
        in_specs=placed,
        out_specs=(rows3, rows3),
        check_vma=False,
    )
```

```python
import jax
import jax.numpy as jnp
from jax import lax
from jax.experimental import pallas as pl
from jax.experimental.pallas import tpu as pltpu
from jax.sharding import PartitionSpec as P

MESH = pl.DeviceIdType.MESH
D = 3584
FF = 256
TOK = 64
CAP = 32
HALF = 128
FULL = 256
COLS = 512
CHUNKS = [slice(c, c + COLS) for c in range(0, D, COLS)]
W_PARTS = 8
Y_BY_Z = ()
G_BY_Z = (0,)
EPS = 1e-06
F32 = jnp.float32
BF16 = jnp.bfloat16

ORDER = [
    "~prepC", "+W0", "+C4", "+W1", "+W2", "+W3", "+W4", "+C1", "~prepF", "+F3", "+F4", "+W5", "+F2",
    "+W6", "+F1", "+W7", "+C2", "?C1", "+C3", "?F3", "+F7", "+C5", "?W0", "?W1", "?F1", "?W2",
    "?F2", "?W3", "+Y3", "+Y2", "?F7", "+Y7", "?C2", "+C6", "?W4", "?C3", "+C7", "?Y3", "?F4",
    "?C4", "?W5", "?W6", "+F6", "?C7", "?C5", "+F5", "?W7", "?C6", "~dhown", "~actown", "~dhoth",
    "+D", "?Y7", "?F6", "+Y6", "~bown", "~ba0", "+BP0", "?D", "~h3", "+H3", "~bs", "+G4", "+G7",
    "?H3", "?Y6", "?Y2", "?F5", "+G5", "~hown", "~fo3", "~h2", "+FP3", "+H2", "+Y1", "?G7", "~ba3",
    "+BP3", "+Y5", "?H2", "+G3", "?FP3", "~fa3", "~fo2", "+FP2", "?G5", "+FD3", "?Y1", "~ba1",
    "+BP1", "?Y5", "~h1", "+H1", "+Y0", "?H1", "?FP2", "+Y4", "?BP3", "+G6", "?G3", "~bb3", "+BD3",
    "~fo1", "?G4", "+FP1", "?BP0", "~fa2", "+FD2", "?FD3", "?Y0", "~gs0", "?Y4", "~h0", "+H0",
    "+G1", "?H0", "?FP1", "~fa1", "?G6", "~ba2", "+G2", "+FD1", "+BP2", "?FD2", "?BP1", "~fo0",
    "+FP0", "?G1", "?BD3", "~bb1", "+BD1", "?BP2", "?FD1", "+G0", "?G2", "~bb2", "+BD2", "?FP0",
    "~fa0", "~cf", "+RF", "?G0", "~bb0", "?BD1", "?BD2", "~cb", "+RB", "?RB", "?RF"
]


def dot(left, right):
    return lax.dot_general(left, right, (((1,), (0,)), ((), ())), preferred_element_type=F32)


def dot_nt(left, right):
    return lax.dot_general(left, right, (((1,), (1,)), ((), ())), preferred_element_type=F32)


def place(slot):
    return 2 * (slot % 4) + slot // 4


def span(position, count=1, base=0):
    return slice(base + position * CAP, base + (position + count) * CAP)


def rows(ref, position, count=1):
    return ref.at[pl.ds(position * CAP, count * CAP), :]


def selection(ids, slot_experts):
    line = lax.broadcasted_iota(jnp.int32, (HALF, TOK), 0)
    slot = lax.shift_right_logical(line, 5)
    rank_of = (line & (CAP - 1)).astype(F32)
    expert = jnp.zeros((HALF, TOK), jnp.int32)
    for s, e in enumerate(slot_experts):
        expert = jnp.where(slot == s, e, expert)
    first = ids[0:1, :] == expert
    second = ids[1:2, :] == expert
    named = jnp.where(first | second, 1.0, 0.0)
    before = lax.broadcasted_iota(jnp.int32, (TOK, TOK), 0) < lax.broadcasted_iota(
        jnp.int32, (TOK, TOK), 1
    )
    ranks = dot(named.astype(BF16), jnp.where(before, 1.0, 0.0).astype(BF16))
    hit = ranks == rank_of
    return first & hit, second & hit


def weigh(masks, weights):
    first, second = masks
    return jnp.where(first, weights[0:1, :], 0.0) + jnp.where(second, weights[1:2, :], 0.0)


def kernel(
    fids, fw, bids, bw, gain, xf_h, xb_h, ct_h, wg_h, wu_h, wd_h, sg_h, su_h,
    nxt, prv,
    xf, xb, ct, wg, wu, wd, wdo, sg, su,
    csend, fsend, crow, frow,
    dho, dsend, drecv, dg, du,
    bsend, brecv, gadd, bown, zsb, zrb, zdb, retb,
    hown, hsend, hrecv, fown, zsf, zrf, zdf, retf,
    fout, gout, dn, b_hot, f_hot,
    ld, s_w, r_w, s_c, r_c, s_f, r_f, s_y, r_y, s_d, r_d, s_g, r_g,
    s_bp, r_bp, s_bd, r_bd, s_h, r_h, s_fp, r_fp, s_fd, r_fd, s_out, r_out,
):
    p = lax.axis_index("pipe")
    me = lax.axis_index("expert")
    z = lax.div(me, 2)
    y = lax.rem(me, 2)
    dz = 2 * lax.rem(z, 2) - 1

    def at_z(zz):
        return lax.rem(zz + 8, 8)

    def dev(zz):
        return (p, at_z(zz) * 2 + y)

    targets = [z, z + dz, z - 2 * dz, z + 3 * dz]
    sources = [z, z + dz, z + 2 * dz, z + 3 * dz]
    pz = z - dz
    z_partner = dev(pz)
    y_partner = (p, z * 2 + 1 - y)
    later = (lax.rem(p + 1, 16), me)
    earlier = (lax.rem(p + 15, 16), me)
    slot_experts = [lax.div(at_z(t), 2) for t in targets]
    block_z = [at_z(s) for s in sources] + [at_z(pz - k * dz) for k in range(4)]

    barrier = pltpu.get_barrier_semaphore()
    friends = [
        z_partner,
        dev(z + dz),
        dev(z + 2 * dz),
        dev(z - 2 * dz),
        dev(z + 3 * dz),
        y_partner,
        later,
        earlier,
    ]
    for friend in friends:
        pl.semaphore_signal(barrier, inc=1, device_id=friend, device_id_type=MESH)

    loads = {}
    for i, (name, src, dst) in enumerate(
        [
            ("ct", ct_h, ct),
            ("xf", xf_h, xf),
            ("wd", wd_h, wd),
            ("wg", wg_h, wg),
            ("wu", wu_h, wu),
            ("sg", sg_h, sg),
            ("su", su_h, su),
            ("xb", xb_h, xb),
        ]
    ):
        loads[name] = pltpu.make_async_copy(src, dst, ld.at[i])
        loads[name].start()

    def need(*names):
        for name in names:
            if name in loads:
                loads.pop(name).wait()

    copies = {}

    def remote(name, src, dst, s_sem, r_sem, target):
        copies[name] = pltpu.make_async_remote_copy(
            src_ref=src, dst_ref=dst, send_sem=s_sem, recv_sem=r_sem,
            device_id=target, device_id_type=MESH,
        )

    part = FF // W_PARTS
    for i in range(W_PARTS):
        cut = pl.ds(i * part, part)
        remote(f"W{i}", wd_h.at[cut, :], wdo.at[cut, :], s_w.at[i], r_w.at[i], y_partner)
    for name, block, out, s_sem, r_sem in (("C", csend, crow, s_c, r_c), ("F", fsend, frow, s_f, r_f)):
        for k in (1, 2, 3):
            remote(
                f"{name}{k}", rows(block, k), rows(out, place(k)), s_sem.at[k], r_sem.at[k], dev(targets[k])
            )
        for k in range(4):
            remote(
                f"{name}{4 + k}", rows(out, place(k)), rows(out, place(4 + k)),
                s_sem.at[4 + k], r_sem.at[4 + k], z_partner,
            )
    for j in range(8):
        if j - 4 in Y_BY_Z:
            remote(
                f"Y{j}", rows(frow, 8 + place(j - 4)), rows(frow, 8 + place(j)), s_y.at[j], r_y.at[j], z_partner
            )
        else:
            remote(f"Y{j}", rows(frow, place(j)), rows(frow, 8 + place(j)), s_y.at[j], r_y.at[j], y_partner)
        if j - 4 in G_BY_Z:
            remote(f"G{j}", rows(bsend, place(j)), rows(gadd, j - 4), s_g.at[j], r_g.at[j], z_partner)
        else:
            remote(f"G{j}", rows(bsend, place(j)), rows(brecv, place(j)), s_g.at[j], r_g.at[j], y_partner)
    remote("D", dsend, drecv, s_d.at[0], r_d.at[0], y_partner)
    for k in range(4):
        remote(f"H{k}", rows(hsend, 2 * k, 2), rows(hrecv, 2 * k, 2), s_h.at[k], r_h.at[k], y_partner)
        remote(f"BP{k}", rows(zsb, k), rows(zrb, k), s_bp.at[k], r_bp.at[k], z_partner)
        remote(f"FP{k}", rows(zsf, k), rows(zrf, k), s_fp.at[k], r_fp.at[k], z_partner)
    for k in (1, 2, 3):
        remote(f"BD{k}", rows(zdb, k), rows(retb, k), s_bd.at[k], r_bd.at[k], dev(sources[k]))
        remote(f"FD{k}", rows(zdf, k), rows(retf, k), s_fd.at[k], r_fd.at[k], dev(sources[k]))
    remote("RF", fout, nxt, s_out.at[0], r_out.at[0], later)
    remote("RB", gout, prv, s_out.at[1], r_out.at[1], earlier)

    computed = {}

    def compute(name, function, *given):
        computed[name] = (function, given)

    def cotangent_blocks():
        masks = selection(bids[...], slot_experts)
        b_hot[...] = weigh(masks, jnp.ones((2, TOK), F32)).T.astype(BF16)
        gather = weigh(masks, bw[...].astype(F32)).astype(BF16)
        need("ct")
        for cs in CHUNKS:
            csend[:, cs] = dot(gather, ct[:, cs]).astype(BF16)
        crow[span(0), :] = csend[span(0), :]
        pl.semaphore_wait(barrier, len(friends))

    def forward_blocks():
        masks = selection(fids[...], slot_experts)
        gather = weigh(masks, jnp.ones((2, TOK), F32)).astype(BF16)
        f_hot[...] = weigh(masks, fw[...].astype(F32)).T.astype(BF16)
        need("xf")
        wide = xf[...].astype(F32)
        scale = lax.rsqrt(jnp.mean(wide * wide, axis=-1, keepdims=True) + EPS)
        fout[...] = (wide * scale * gain[...].astype(F32)).astype(BF16)
        for cs in CHUNKS:
            fsend[:, cs] = dot(gather, fout[:, cs]).astype(BF16)
        frow[span(0), :] = fsend[span(0), :]

    def own_d_hidden():
        need("wd")
        dho[...] = dot_nt(crow[...], wd[...])

    def other_d_hidden():
        dsend[...] = dot_nt(crow[...], wdo[...]).astype(BF16)

    def activation_grad(j, column, d_hidden):
        need("sg", "su")
        start = pl.multiple_of((block_z[j] * 2 + column) * CAP, CAP)
        gate_b = sg[pl.ds(start, CAP), :].astype(F32)
        up_b = su[pl.ds(start, CAP), :].astype(F32)
        sigmoid = jax.nn.sigmoid(gate_b)
        d_gate = d_hidden * up_b * sigmoid * (1.0 + gate_b * (1.0 - sigmoid))
        d_up = d_hidden * gate_b * sigmoid
        return d_gate.astype(BF16), d_up.astype(BF16)

    def own_activation():
        for j in range(8):
            js = span(place(j))
            dg[js, :], du[js, :] = activation_grad(j, y, dho[js, :])

    def other_gradient():
        need("wg", "wu")
        for j in range(8):
            js = span(place(j))
            ks = span(place(j), 1, FULL)
            dg[ks, :], du[ks, :] = activation_grad(j, 1 - y, drecv[js, :].astype(F32))
        for cs in CHUNKS:
            total = dot_nt(dg[FULL:, :], wg[cs, :]) + dot_nt(du[FULL:, :], wu[cs, :])
            bsend[:, cs] = total.astype(BF16)

    def own_gradient():
        need("wg", "wu")
        for cs in CHUNKS:
            bown[:, cs] = dot_nt(dg[0:FULL, :], wg[cs, :]) + dot_nt(du[0:FULL, :], wu[cs, :])

    def hidden(block):
        need("wg", "wu")
        gate = dot(block, wg[...])
        up = dot(block, wu[...])
        return (gate * jax.nn.sigmoid(gate) * up).astype(BF16)

    def own_hidden():
        hown[...] = hidden(frow[0:FULL, :])

    def other_hidden(k):
        hsend[span(2 * k, 2), :] = hidden(frow[span(2 * k, 2, FULL), :])

    def forward_partial(k):
        need("wd")
        ks = span(2 * k, 2)
        for cs in CHUNKS:
            total = dot(hown[ks, :], wd[:, cs]) + dot(hrecv[ks, :], wdo[:, cs])
            fown[span(k), cs] = total[0:CAP, :]
            zsf[span(k), cs] = total[CAP:, :].astype(BF16)

    def forward_sum(k):
        total = (fown[span(k), :] + zrf[span(k), :].astype(F32)).astype(BF16)
        out = zdf if k else retf
        out[span(k), :] = total

    def gradient_across(k):
        js = span(place(k))
        bsend[js, :] = (bsend[js, :].astype(F32) + gadd[span(k), :].astype(F32)).astype(BF16)

    def gradient_partial(k):
        js = span(place(4 + k))
        total = bown[js, :]
        if k not in G_BY_Z:
            total = total + brecv[js, :].astype(F32)
        zsb[span(k), :] = total.astype(BF16)

    def gradient_sum(k):
        js = span(place(k))
        total = bown[js, :] + brecv[js, :].astype(F32) + zrb[span(k), :].astype(F32)
        out = zdb if k else retb
        out[span(k), :] = total.astype(BF16)

    def forward_out():
        for cs in CHUNKS:
            fout[:, cs] = (xf[:, cs].astype(F32) + dot(f_hot[...], retf[:, cs])).astype(BF16)

    def gradient_out():
        need("xb")
        wide_b = xb[...].astype(F32)
        scale_b = lax.rsqrt(jnp.mean(wide_b * wide_b, axis=-1, keepdims=True) + EPS)
        gain_wide = gain[...].astype(F32)
        inner = jnp.zeros((TOK, 1), F32)
        for cs in CHUNKS:
            d_unit = dot(b_hot[...], retb[:, cs]) * gain_wide[:, cs]
            dn[:, cs] = d_unit
            inner = inner + jnp.sum(d_unit * (xb[:, cs].astype(F32) * scale_b), axis=-1, keepdims=True)
        inner = inner * (1.0 / D)
        for cs in CHUNKS:
            unit = xb[:, cs].astype(F32) * scale_b
            gout[:, cs] = (ct[:, cs].astype(F32) + scale_b * (dn[:, cs] - unit * inner)).astype(BF16)

    compute("prepC", cotangent_blocks)
    compute("prepF", forward_blocks)
    compute("dhown", own_d_hidden)
    compute("dhoth", other_d_hidden)
    compute("actown", own_activation)
    compute("bs", other_gradient)
    compute("bown", own_gradient)
    compute("hown", own_hidden)
    compute("cf", forward_out)
    compute("cb", gradient_out)
    for k in range(4):
        compute(f"h{k}", other_hidden, k)
        compute(f"fo{k}", forward_partial, k)
        compute(f"fa{k}", forward_sum, k)
        compute(f"gs{k}", gradient_across, k)
        compute(f"ba{k}", gradient_partial, k)
        compute(f"bb{k}", gradient_sum, k)

    sent = []
    for step in ORDER:
        kind, name = step[0], step[1:]
        if kind == "~":
            function, given = computed[name]
            function(*given)
        elif name == "RF":
            if kind == "+":
                pl.when(p < 15)(copies[name].start)
            else:
                pl.when(p > 0)(copies[name].wait_recv)
        elif name == "RB":
            if kind == "+":
                pl.when(p > 0)(copies[name].start)
            else:
                pl.when(p < 15)(copies[name].wait_recv)
        elif kind == "+":
            copies[name].start()
            sent.append(name)
        else:
            copies[name].wait_recv()

    @pl.when(p == 0)
    def _():
        gout[...] = jnp.zeros_like(gout)
        zero = pltpu.make_async_copy(gout, nxt, ld.at[8])
        zero.start()
        zero.wait()

    @pl.when(p == 15)
    def _():
        fout[...] = jnp.zeros_like(fout)
        zero = pltpu.make_async_copy(fout, prv, ld.at[9])
        zero.start()
        zero.wait()

    for name in sent:
        copies[name].wait_send()
    pl.when(p < 15)(copies["RF"].wait_send)
    pl.when(p > 0)(copies["RB"].wait_send)


def hand_over(first, second, first_out, second_out, held, in_sem, out_sem):
    cut = TOK // 2
    steps = []
    for i, (src, dst) in enumerate(((first, first_out), (second, second_out))):
        for j in range(2):
            here = pl.ds(j * cut, cut)
            steps.append(
                (
                    pltpu.make_async_copy(src.at[here, :], held.at[i, here, :], in_sem.at[i, j]),
                    pltpu.make_async_copy(held.at[i, here, :], dst.at[here, :], out_sem.at[i, j]),
                )
            )
    for arrive, _ in steps:
        arrive.start()
    for arrive, leave in steps:
        arrive.wait()
        leave.start()
    for _, leave in steps:
        leave.wait()


def body(
    fwd_rows,
    fwd_experts,
    fwd_weight,
    back_rows,
    back_experts,
    back_weight,
    back_cotangent,
    norm_gain,
    w_gate,
    w_up,
    w_down,
    saved_gate,
    saved_up,
):
    vmem = pl.BlockSpec(memory_space=pltpu.VMEM)
    hbm = pl.BlockSpec(memory_space=pl.ANY)
    dma = pltpu.SemaphoreType.DMA
    out_shape = (jax.ShapeDtypeStruct((TOK, D), BF16), jax.ShapeDtypeStruct((TOK, D), BF16))

    def wide(count, kind=BF16):
        return pltpu.VMEM((count, D), kind)

    def narrow(count, kind=BF16):
        return pltpu.VMEM((count, FF), kind)

    outs = pl.pallas_call(
        kernel,
        out_shape=out_shape,
        in_specs=[vmem] * 5 + [hbm] * 8,
        out_specs=(hbm, hbm),
        scratch_shapes=[
            wide(TOK), wide(TOK), wide(TOK),
            narrow(D), narrow(D), wide(FF), wide(FF), narrow(512), narrow(512),
            wide(HALF), wide(HALF), wide(FULL), wide(2 * FULL),
            narrow(FULL, F32), narrow(FULL), narrow(FULL), narrow(512), narrow(512),
            wide(FULL), wide(FULL), wide(HALF), wide(FULL, F32), wide(HALF), wide(HALF), wide(HALF), wide(HALF),
            narrow(FULL), narrow(FULL), narrow(FULL), wide(HALF, F32), wide(HALF), wide(HALF), wide(HALF),
            wide(HALF),
            wide(TOK), wide(TOK), wide(TOK, F32),
            pltpu.VMEM((TOK, HALF), BF16), pltpu.VMEM((TOK, HALF), BF16),
            dma((10,)), dma((W_PARTS,)), dma((W_PARTS,)), dma((8,)), dma((8,)), dma((8,)), dma((8,)),
            dma((8,)), dma((8,)), dma((1,)), dma((1,)), dma((8,)), dma((8,)),
            dma((4,)), dma((4,)), dma((4,)), dma((4,)), dma((4,)), dma((4,)),
            dma((4,)), dma((4,)), dma((4,)), dma((4,)), dma((2,)), dma((2,)),
        ],
        compiler_params=pltpu.CompilerParams(
            collective_id=0, has_side_effects=True, vmem_limit_bytes=56 * 2**20
        ),
        cost_estimate=pl.CostEstimate(flops=5_700_000_000, bytes_accessed=10_000_000, transcendentals=400_000),
    )(
        fwd_experts[0].T,
        fwd_weight[0].T,
        back_experts[0].T,
        back_weight[0].T,
        norm_gain,
        fwd_rows[0],
        back_rows[0],
        back_cotangent[0],
        w_gate[0, 0],
        w_up[0, 0],
        w_down[0, 0],
        saved_gate[0, 0],
        saved_up[0, 0],
    )
    outs = pl.pallas_call(
        hand_over,
        out_shape=out_shape,
        in_specs=[hbm, hbm],
        out_specs=(hbm, hbm),
        scratch_shapes=[pltpu.VMEM((2, TOK, D), BF16), dma((2, 2)), dma((2, 2))],
        compiler_params=pltpu.CompilerParams(vmem_limit_bytes=56 * 2**20),
    )(*outs)
    return outs[0][None], outs[1][None]


def solution(mesh):
    rows3 = P("pipe", "expert", None)
    rows4 = P("pipe", "expert", None, None)
    placed = (rows3,) * 7 + (P("pipe", None),) + (rows4,) * 5
    return jax.shard_map(
        body,
        mesh=mesh,
        in_specs=placed,
        out_specs=(rows3, rows3),
        check_vma=False,
    )
```

```python
import jax
import jax.numpy as jnp
from jax import lax
from jax.experimental import pallas as pl
from jax.experimental.pallas import tpu as pltpu
from jax.sharding import PartitionSpec as P

MESH = pl.DeviceIdType.MESH
D = 3584
FF = 256
TOK = 64
CAP = 32
HALF = 128
FULL = 256
COLS = 512
CHUNKS = [slice(c, c + COLS) for c in range(0, D, COLS)]
W_PARTS = 8
Y_BY_Z = ()
G_BY_Z = (1,)
EPS = 1e-06
F32 = jnp.float32
BF16 = jnp.bfloat16

ORDER = [
    "~enter", "+F3", "+W0", "+W1", "+F4", "+C4", "+W2", "+W3", "+W4", "+C2", "+W5", "+W6", "?W0",
    "+F1", "?F3", "+F7", "+F2", "?W1", "+C3", "+Y3", "?F1", "+F5", "?W2", "?C2", "?F7", "+Y7",
    "+C6", "?F2", "+W7", "+F6", "?C3", "?Y3", "+C1", "+C7", "?F4", "?F5", "+Y1", "?Y7", "~h3",
    "+H3", "?W3", "?C1", "+C5", "?F6", "?W4", "~hown", "+Y5", "?Y1", "?W5", "?W6", "?C4", "?H3",
    "?W7", "~fo3", "+FP3", "?C6", "+Y2", "?C5", "?C7", "~dhown", "~actown", "~bown", "~ba1", "+BP1",
    "?Y5", "~h1", "+H1", "+Y6", "?FP3", "~fa3", "+FD3", "?Y2", "~dhoth", "?H1", "+D", "~fo1",
    "+FP1", "?Y6", "+Y4", "~h2", "?D", "~bs", "+H2", "+G5", "+G7", "+Y0", "?H2", "~fo2", "+FP2",
    "?G7", "~ba3", "+BP3", "?FP1", "~fa1", "+G6", "?BP1", "+FD1", "?Y4", "?Y0", "~h0", "+H0", "+G3",
    "?FP2", "~fa2", "+FD2", "?G6", "~ba2", "?H0", "+BP2", "+G2", "?BP3", "+G4", "?G5", "?G3",
    "~bb3", "+BD3", "~fo0", "+FP0", "?G2", "~gs1", "+G1", "?BP2", "~bb2", "+BD2", "?G4", "~ba0",
    "+G0", "+BP0", "?FD3", "?FP0", "?FD2", "?BD3", "~fa0", "?FD1", "~cf", "?G1", "~bb1", "+BD1",
    "+RF", "?BP0", "?G0", "~bb0", "?BD1", "?BD2", "~cb", "+RB", "?RF", "?RB"
]


def dot(left, right):
    return lax.dot_general(left, right, (((1,), (0,)), ((), ())), preferred_element_type=F32)


def dot_nt(left, right):
    return lax.dot_general(left, right, (((1,), (1,)), ((), ())), preferred_element_type=F32)


def place(slot):
    return 2 * (slot % 4) + slot // 4


def span(position, count=1, base=0):
    return slice(base + position * CAP, base + (position + count) * CAP)


def rows(ref, position, count=1):
    return ref.at[pl.ds(position * CAP, count * CAP), :]


def selection(ids, slot_experts):
    line = lax.broadcasted_iota(jnp.int32, (HALF, TOK), 0)
    slot = lax.shift_right_logical(line, 5)
    rank_of = (line & (CAP - 1)).astype(F32)
    expert = jnp.zeros((HALF, TOK), jnp.int32)
    for s, e in enumerate(slot_experts):
        expert = jnp.where(slot == s, e, expert)
    first = ids[0:1, :] == expert
    second = ids[1:2, :] == expert
    named = jnp.where(first | second, 1.0, 0.0)
    before = lax.broadcasted_iota(jnp.int32, (TOK, TOK), 0) < lax.broadcasted_iota(
        jnp.int32, (TOK, TOK), 1
    )
    ranks = dot(named.astype(BF16), jnp.where(before, 1.0, 0.0).astype(BF16))
    hit = ranks == rank_of
    return first & hit, second & hit


def weigh(masks, weights):
    first, second = masks
    return jnp.where(first, weights[0:1, :], 0.0) + jnp.where(second, weights[1:2, :], 0.0)


def kernel(
    fids, fw, bids, bw, gain, xf_h, xb_h, ct_h, wg_h, wu_h, wd_h, sg_h, su_h,
    nxt, prv,
    xf, xb, ct, wg, wu, wd, wdo, sg, su,
    csend, fsend, crow, frow,
    dho, dsend, drecv, dg, du,
    bsend, brecv, gadd, bown, zsb, zrb, zdb, retb,
    hown, hsend, hrecv, fown, zsf, zrf, zdf, retf,
    fout, gout, dn, b_hot, f_hot,
    ld, s_w, r_w, s_c, r_c, s_f, r_f, s_y, r_y, s_d, r_d, s_g, r_g,
    s_bp, r_bp, s_bd, r_bd, s_h, r_h, s_fp, r_fp, s_fd, r_fd, s_out, r_out,
):
    p = lax.axis_index("pipe")
    me = lax.axis_index("expert")
    z = lax.div(me, 2)
    y = lax.rem(me, 2)
    dz = 2 * lax.rem(z, 2) - 1

    def at_z(zz):
        return lax.rem(zz + 8, 8)

    def dev(zz):
        return (p, at_z(zz) * 2 + y)

    targets = [z, z + dz, z - 2 * dz, z + 3 * dz]
    sources = [z, z + dz, z + 2 * dz, z + 3 * dz]
    pz = z - dz
    z_partner = dev(pz)
    y_partner = (p, z * 2 + 1 - y)
    later = (lax.rem(p + 1, 16), me)
    earlier = (lax.rem(p + 15, 16), me)
    slot_experts = [lax.div(at_z(t), 2) for t in targets]
    block_z = [at_z(s) for s in sources] + [at_z(pz - k * dz) for k in range(4)]

    barrier = pltpu.get_barrier_semaphore()
    friends = [
        z_partner,
        dev(z + dz),
        dev(z + 2 * dz),
        dev(z - 2 * dz),
        dev(z + 3 * dz),
        y_partner,
        later,
        earlier,
    ]
    for friend in friends:
        pl.semaphore_signal(barrier, inc=1, device_id=friend, device_id_type=MESH)

    loads = {}
    for i, (name, src, dst) in enumerate(
        [
            ("ct", ct_h, ct),
            ("xf", xf_h, xf),
            ("wd", wd_h, wd),
            ("wg", wg_h, wg),
            ("wu", wu_h, wu),
            ("sg", sg_h, sg),
            ("su", su_h, su),
            ("xb", xb_h, xb),
        ]
    ):
        loads[name] = pltpu.make_async_copy(src, dst, ld.at[i])
        loads[name].start()

    def need(*names):
        for name in names:
            if name in loads:
                loads.pop(name).wait()

    copies = {}

    def remote(name, src, dst, s_sem, r_sem, target):
        copies[name] = pltpu.make_async_remote_copy(
            src_ref=src, dst_ref=dst, send_sem=s_sem, recv_sem=r_sem,
            device_id=target, device_id_type=MESH,
        )

    part = FF // W_PARTS
    for i in range(W_PARTS):
        cut = pl.ds(i * part, part)
        remote(f"W{i}", wd_h.at[cut, :], wdo.at[cut, :], s_w.at[i], r_w.at[i], y_partner)
    for name, block, out, s_sem, r_sem in (("C", csend, crow, s_c, r_c), ("F", fsend, frow, s_f, r_f)):
        for k in (1, 2, 3):
            remote(
                f"{name}{k}", rows(block, k), rows(out, place(k)), s_sem.at[k], r_sem.at[k], dev(targets[k])
            )
        for k in range(4):
            remote(
                f"{name}{4 + k}", rows(out, place(k)), rows(out, place(4 + k)),
                s_sem.at[4 + k], r_sem.at[4 + k], z_partner,
            )
    for j in range(8):
        if j - 4 in Y_BY_Z:
            remote(
                f"Y{j}", rows(frow, 8 + place(j - 4)), rows(frow, 8 + place(j)), s_y.at[j], r_y.at[j], z_partner
            )
        else:
            remote(f"Y{j}", rows(frow, place(j)), rows(frow, 8 + place(j)), s_y.at[j], r_y.at[j], y_partner)
        if j - 4 in G_BY_Z:
            remote(f"G{j}", rows(bsend, place(j)), rows(gadd, j - 4), s_g.at[j], r_g.at[j], z_partner)
        else:
            remote(f"G{j}", rows(bsend, place(j)), rows(brecv, place(j)), s_g.at[j], r_g.at[j], y_partner)
    remote("D", dsend, drecv, s_d.at[0], r_d.at[0], y_partner)
    for k in range(4):
        remote(f"H{k}", rows(hsend, 2 * k, 2), rows(hrecv, 2 * k, 2), s_h.at[k], r_h.at[k], y_partner)
        remote(f"BP{k}", rows(zsb, k), rows(zrb, k), s_bp.at[k], r_bp.at[k], z_partner)
        remote(f"FP{k}", rows(zsf, k), rows(zrf, k), s_fp.at[k], r_fp.at[k], z_partner)
    for k in (1, 2, 3):
        remote(f"BD{k}", rows(zdb, k), rows(retb, k), s_bd.at[k], r_bd.at[k], dev(sources[k]))
        remote(f"FD{k}", rows(zdf, k), rows(retf, k), s_fd.at[k], r_fd.at[k], dev(sources[k]))
    remote("RF", fout, nxt, s_out.at[0], r_out.at[0], later)
    remote("RB", gout, prv, s_out.at[1], r_out.at[1], earlier)

    computed = {}

    def compute(name, function, *given):
        computed[name] = (function, given)

    def cotangent_blocks():
        masks = selection(bids[...], slot_experts)
        b_hot[...] = weigh(masks, jnp.ones((2, TOK), F32)).T.astype(BF16)
        gather = weigh(masks, bw[...].astype(F32)).astype(BF16)
        need("ct")
        for cs in CHUNKS:
            csend[:, cs] = dot(gather, ct[:, cs]).astype(BF16)
        crow[span(0), :] = csend[span(0), :]

    def forward_blocks():
        masks = selection(fids[...], slot_experts)
        gather = weigh(masks, jnp.ones((2, TOK), F32)).astype(BF16)
        f_hot[...] = weigh(masks, fw[...].astype(F32)).T.astype(BF16)
        need("xf")
        wide = xf[...].astype(F32)
        scale = lax.rsqrt(jnp.mean(wide * wide, axis=-1, keepdims=True) + EPS)
        fout[...] = (wide * scale * gain[...].astype(F32)).astype(BF16)
        for cs in CHUNKS:
            fsend[:, cs] = dot(gather, fout[:, cs]).astype(BF16)
        frow[span(0), :] = fsend[span(0), :]

    def enter():
        pl.semaphore_wait(barrier, len(friends))

    def own_d_hidden():
        need("wd")
        dho[...] = dot_nt(crow[...], wd[...])

    def other_d_hidden():
        dsend[...] = dot_nt(crow[...], wdo[...]).astype(BF16)

    def activation_grad(j, column, d_hidden):
        need("sg", "su")
        start = pl.multiple_of((block_z[j] * 2 + column) * CAP, CAP)
        gate_b = sg[pl.ds(start, CAP), :].astype(F32)
        up_b = su[pl.ds(start, CAP), :].astype(F32)
        sigmoid = jax.nn.sigmoid(gate_b)
        d_gate = d_hidden * up_b * sigmoid * (1.0 + gate_b * (1.0 - sigmoid))
        d_up = d_hidden * gate_b * sigmoid
        return d_gate.astype(BF16), d_up.astype(BF16)

    def own_activation():
        for j in range(8):
            js = span(place(j))
            dg[js, :], du[js, :] = activation_grad(j, y, dho[js, :])

    def other_gradient():
        need("wg", "wu")
        for j in range(8):
            js = span(place(j))
            ks = span(place(j), 1, FULL)
            dg[ks, :], du[ks, :] = activation_grad(j, 1 - y, drecv[js, :].astype(F32))
        for cs in CHUNKS:
            total = dot_nt(dg[FULL:, :], wg[cs, :]) + dot_nt(du[FULL:, :], wu[cs, :])
            bsend[:, cs] = total.astype(BF16)

    def own_gradient():
        need("wg", "wu")
        for cs in CHUNKS:
            bown[:, cs] = dot_nt(dg[0:FULL, :], wg[cs, :]) + dot_nt(du[0:FULL, :], wu[cs, :])

    def hidden(block):
        need("wg", "wu")
        gate = dot(block, wg[...])
        up = dot(block, wu[...])
        return (gate * jax.nn.sigmoid(gate) * up).astype(BF16)

    def own_hidden():
        hown[...] = hidden(frow[0:FULL, :])

    def other_hidden(k):
        hsend[span(2 * k, 2), :] = hidden(frow[span(2 * k, 2, FULL), :])

    def forward_partial(k):
        need("wd")
        ks = span(2 * k, 2)
        for cs in CHUNKS:
            total = dot(hown[ks, :], wd[:, cs]) + dot(hrecv[ks, :], wdo[:, cs])
            fown[span(k), cs] = total[0:CAP, :]
            zsf[span(k), cs] = total[CAP:, :].astype(BF16)

    def forward_sum(k):
        total = (fown[span(k), :] + zrf[span(k), :].astype(F32)).astype(BF16)
        out = zdf if k else retf
        out[span(k), :] = total

    def gradient_across(k):
        js = span(place(k))
        bsend[js, :] = (bsend[js, :].astype(F32) + gadd[span(k), :].astype(F32)).astype(BF16)

    def gradient_partial(k):
        js = span(place(4 + k))
        total = bown[js, :]
        if k not in G_BY_Z:
            total = total + brecv[js, :].astype(F32)
        zsb[span(k), :] = total.astype(BF16)

    def gradient_sum(k):
        js = span(place(k))
        total = bown[js, :] + brecv[js, :].astype(F32) + zrb[span(k), :].astype(F32)
        out = zdb if k else retb
        out[span(k), :] = total.astype(BF16)

    def forward_out():
        for cs in CHUNKS:
            fout[:, cs] = (xf[:, cs].astype(F32) + dot(f_hot[...], retf[:, cs])).astype(BF16)

    def gradient_out():
        need("xb")
        wide_b = xb[...].astype(F32)
        scale_b = lax.rsqrt(jnp.mean(wide_b * wide_b, axis=-1, keepdims=True) + EPS)
        gain_wide = gain[...].astype(F32)
        inner = jnp.zeros((TOK, 1), F32)
        for cs in CHUNKS:
            d_unit = dot(b_hot[...], retb[:, cs]) * gain_wide[:, cs]
            dn[:, cs] = d_unit
            inner = inner + jnp.sum(d_unit * (xb[:, cs].astype(F32) * scale_b), axis=-1, keepdims=True)
        inner = inner * (1.0 / D)
        for cs in CHUNKS:
            unit = xb[:, cs].astype(F32) * scale_b
            gout[:, cs] = (ct[:, cs].astype(F32) + scale_b * (dn[:, cs] - unit * inner)).astype(BF16)

    compute("enter", enter)
    compute("dhown", own_d_hidden)
    compute("dhoth", other_d_hidden)
    compute("actown", own_activation)
    compute("bs", other_gradient)
    compute("bown", own_gradient)
    compute("hown", own_hidden)
    compute("cf", forward_out)
    compute("cb", gradient_out)
    for k in range(4):
        compute(f"h{k}", other_hidden, k)
        compute(f"fo{k}", forward_partial, k)
        compute(f"fa{k}", forward_sum, k)
        compute(f"gs{k}", gradient_across, k)
        compute(f"ba{k}", gradient_partial, k)
        compute(f"bb{k}", gradient_sum, k)

    cotangent_blocks()
    forward_blocks()
    sent = []
    for step in ORDER:
        kind, name = step[0], step[1:]
        if kind == "~":
            function, given = computed[name]
            function(*given)
        elif name == "RF":
            if kind == "+":
                pl.when(p < 15)(copies[name].start)
            else:
                pl.when(p > 0)(copies[name].wait_recv)
        elif name == "RB":
            if kind == "+":
                pl.when(p > 0)(copies[name].start)
            else:
                pl.when(p < 15)(copies[name].wait_recv)
        elif kind == "+":
            copies[name].start()
            sent.append(name)
        else:
            copies[name].wait_recv()

    @pl.when(p == 0)
    def _():
        gout[...] = jnp.zeros_like(gout)
        zero = pltpu.make_async_copy(gout, nxt, ld.at[8])
        zero.start()
        zero.wait()

    @pl.when(p == 15)
    def _():
        fout[...] = jnp.zeros_like(fout)
        zero = pltpu.make_async_copy(fout, prv, ld.at[9])
        zero.start()
        zero.wait()

    for name in sent:
        copies[name].wait_send()
    pl.when(p < 15)(copies["RF"].wait_send)
    pl.when(p > 0)(copies["RB"].wait_send)


def hand_over(first, second, first_out, second_out, held, in_sem, out_sem):
    cut = TOK // 2
    steps = []
    for i, (src, dst) in enumerate(((first, first_out), (second, second_out))):
        for j in range(2):
            here = pl.ds(j * cut, cut)
            steps.append(
                (
                    pltpu.make_async_copy(src.at[here, :], held.at[i, here, :], in_sem.at[i, j]),
                    pltpu.make_async_copy(held.at[i, here, :], dst.at[here, :], out_sem.at[i, j]),
                )
            )
    for arrive, _ in steps:
        arrive.start()
    for arrive, leave in steps:
        arrive.wait()
        leave.start()
    for _, leave in steps:
        leave.wait()


def body(
    fwd_rows,
    fwd_experts,
    fwd_weight,
    back_rows,
    back_experts,
    back_weight,
    back_cotangent,
    norm_gain,
    w_gate,
    w_up,
    w_down,
    saved_gate,
    saved_up,
):
    vmem = pl.BlockSpec(memory_space=pltpu.VMEM)
    hbm = pl.BlockSpec(memory_space=pl.ANY)
    dma = pltpu.SemaphoreType.DMA
    out_shape = (jax.ShapeDtypeStruct((TOK, D), BF16), jax.ShapeDtypeStruct((TOK, D), BF16))

    def wide(count, kind=BF16):
        return pltpu.VMEM((count, D), kind)

    def narrow(count, kind=BF16):
        return pltpu.VMEM((count, FF), kind)

    outs = pl.pallas_call(
        kernel,
        out_shape=out_shape,
        in_specs=[vmem] * 5 + [hbm] * 8,
        out_specs=(hbm, hbm),
        scratch_shapes=[
            wide(TOK), wide(TOK), wide(TOK),
            narrow(D), narrow(D), wide(FF), wide(FF), narrow(512), narrow(512),
            wide(HALF), wide(HALF), wide(FULL), wide(2 * FULL),
            narrow(FULL, F32), narrow(FULL), narrow(FULL), narrow(512), narrow(512),
            wide(FULL), wide(FULL), wide(HALF), wide(FULL, F32), wide(HALF), wide(HALF), wide(HALF), wide(HALF),
            narrow(FULL), narrow(FULL), narrow(FULL), wide(HALF, F32), wide(HALF), wide(HALF), wide(HALF),
            wide(HALF),
            wide(TOK), wide(TOK), wide(TOK, F32),
            pltpu.VMEM((TOK, HALF), BF16), pltpu.VMEM((TOK, HALF), BF16),
            dma((10,)), dma((W_PARTS,)), dma((W_PARTS,)), dma((8,)), dma((8,)), dma((8,)), dma((8,)),
            dma((8,)), dma((8,)), dma((1,)), dma((1,)), dma((8,)), dma((8,)),
            dma((4,)), dma((4,)), dma((4,)), dma((4,)), dma((4,)), dma((4,)),
            dma((4,)), dma((4,)), dma((4,)), dma((4,)), dma((2,)), dma((2,)),
        ],
        compiler_params=pltpu.CompilerParams(
            collective_id=0, has_side_effects=True, vmem_limit_bytes=56 * 2**20
        ),
        cost_estimate=pl.CostEstimate(flops=5_700_000_000, bytes_accessed=10_000_000, transcendentals=400_000),
    )(
        fwd_experts[0].T,
        fwd_weight[0].T,
        back_experts[0].T,
        back_weight[0].T,
        norm_gain,
        fwd_rows[0],
        back_rows[0],
        back_cotangent[0],
        w_gate[0, 0],
        w_up[0, 0],
        w_down[0, 0],
        saved_gate[0, 0],
        saved_up[0, 0],
    )
    outs = pl.pallas_call(
        hand_over,
        out_shape=out_shape,
        in_specs=[hbm, hbm],
        out_specs=(hbm, hbm),
        scratch_shapes=[pltpu.VMEM((2, TOK, D), BF16), dma((2, 2)), dma((2, 2))],
        compiler_params=pltpu.CompilerParams(vmem_limit_bytes=56 * 2**20),
    )(*outs)
    return outs[0][None], outs[1][None]


def solution(mesh):
    rows3 = P("pipe", "expert", None)
    rows4 = P("pipe", "expert", None, None)
    placed = (rows3,) * 7 + (P("pipe", None),) + (rows4,) * 5
    return jax.shard_map(
        body,
        mesh=mesh,
        in_specs=placed,
        out_specs=(rows3, rows3),
        check_vma=False,
    )
```

```python
import jax
import jax.numpy as jnp
from jax import lax
from jax.experimental import pallas as pl
from jax.experimental.pallas import tpu as pltpu
from jax.sharding import PartitionSpec as P

MESH = pl.DeviceIdType.MESH
D = 3584
FF = 256
TOK = 64
CAP = 32
HALF = 128
FULL = 256
COLS = 512
CHUNKS = [slice(c, c + COLS) for c in range(0, D, COLS)]
W_PARTS = 8
Y_BY_Z = ()
G_BY_Z = (0,)
EPS = 1e-06
F32 = jnp.float32
BF16 = jnp.bfloat16

ORDER = [
    "~enter", "+C2", "+F1", "+F3", "+C1", "+W0", "+C4", "+W1", "+W2", "?C2", "+W3", "+C6", "?W0",
    "?F1", "+F5", "+W4", "+W5", "+C3", "?C6", "?F3", "+Y3", "+F7", "+W6", "?F5", "?W1", "?W2",
    "?C1", "+F2", "?W3", "+C5", "?W4", "+Y5", "?C3", "?W5", "?Y3", "+C7", "?F7", "?C4", "+Y1",
    "+W7", "+Y7", "+F4", "?F2", "+F6", "?C7", "?C5", "~dhown", "~actown", "?Y1", "~bown", "?Y5",
    "~ba0", "?W6", "~h1", "+H1", "?W7", "+BP0", "~dhoth", "+D", "?F4", "?F6", "~hown", "?Y7", "~h3",
    "+H3", "+Y2", "?H1", "~fo1", "+FP1", "?D", "~bs", "+G7", "+Y6", "?H3", "~fo3", "+FP3", "+G4",
    "?FP3", "?G7", "+G3", "~fa3", "+FD3", "~ba3", "+BP3", "?Y2", "?Y6", "~h2", "?FP1", "~fa1",
    "+H2", "+G5", "+G6", "?H2", "~fo2", "+Y0", "+FP2", "?G5", "~ba1", "?BP3", "+FD1", "+BP1", "+Y4",
    "?G6", "+G1", "?FP2", "~fa2", "~ba2", "+FD2", "?G3", "~bb3", "+BD3", "?G4", "?FD3", "+BP2",
    "?Y0", "?Y4", "~h0", "+H0", "+G2", "?H0", "?G1", "?FD2", "?BP1", "~gs0", "~bb1", "+G0", "+BD1",
    "~fo0", "+FP0", "?G2", "?BP2", "~bb2", "?FD1", "+BD2", "?BP0", "?FP0", "~fa0", "~cf", "+RF",
    "?G0", "~bb0", "?BD2", "?BD1", "?BD3", "~cb", "+RB", "?RB", "?RF"
]


def dot(left, right):
    return lax.dot_general(left, right, (((1,), (0,)), ((), ())), preferred_element_type=F32)


def dot_nt(left, right):
    return lax.dot_general(left, right, (((1,), (1,)), ((), ())), preferred_element_type=F32)


def place(slot):
    return 2 * (slot % 4) + slot // 4


def span(position, count=1, base=0):
    return slice(base + position * CAP, base + (position + count) * CAP)


def rows(ref, position, count=1):
    return ref.at[pl.ds(position * CAP, count * CAP), :]


def selection(ids, slot_experts):
    line = lax.broadcasted_iota(jnp.int32, (HALF, TOK), 0)
    slot = lax.shift_right_logical(line, 5)
    rank_of = (line & (CAP - 1)).astype(F32)
    expert = jnp.zeros((HALF, TOK), jnp.int32)
    for s, e in enumerate(slot_experts):
        expert = jnp.where(slot == s, e, expert)
    first = ids[0:1, :] == expert
    second = ids[1:2, :] == expert
    named = jnp.where(first | second, 1.0, 0.0)
    before = lax.broadcasted_iota(jnp.int32, (TOK, TOK), 0) < lax.broadcasted_iota(
        jnp.int32, (TOK, TOK), 1
    )
    ranks = dot(named.astype(BF16), jnp.where(before, 1.0, 0.0).astype(BF16))
    hit = ranks == rank_of
    return first & hit, second & hit


def weigh(masks, weights):
    first, second = masks
    return jnp.where(first, weights[0:1, :], 0.0) + jnp.where(second, weights[1:2, :], 0.0)


def kernel(
    fids, fw, bids, bw, gain, xf_h, xb_h, ct_h, wg_h, wu_h, wd_h, sg_h, su_h,
    nxt, prv,
    xf, xb, ct, wg, wu, wd, wdo, sg, su,
    csend, fsend, crow, frow,
    dho, dsend, drecv, dg, du,
    bsend, brecv, gadd, bown, zsb, zrb, zdb, retb,
    hown, hsend, hrecv, fown, zsf, zrf, zdf, retf,
    fout, gout, dn, b_hot, f_hot,
    ld, s_w, r_w, s_c, r_c, s_f, r_f, s_y, r_y, s_d, r_d, s_g, r_g,
    s_bp, r_bp, s_bd, r_bd, s_h, r_h, s_fp, r_fp, s_fd, r_fd, s_out, r_out,
):
    p = lax.axis_index("pipe")
    me = lax.axis_index("expert")
    z = lax.div(me, 2)
    y = lax.rem(me, 2)
    dz = 2 * lax.rem(z, 2) - 1

    def at_z(zz):
        return lax.rem(zz + 8, 8)

    def dev(zz):
        return (p, at_z(zz) * 2 + y)

    targets = [z, z + dz, z - 2 * dz, z + 3 * dz]
    sources = [z, z + dz, z + 2 * dz, z + 3 * dz]
    pz = z - dz
    z_partner = dev(pz)
    y_partner = (p, z * 2 + 1 - y)
    later = (lax.rem(p + 1, 16), me)
    earlier = (lax.rem(p + 15, 16), me)
    slot_experts = [lax.div(at_z(t), 2) for t in targets]
    block_z = [at_z(s) for s in sources] + [at_z(pz - k * dz) for k in range(4)]

    barrier = pltpu.get_barrier_semaphore()
    friends = [
        z_partner,
        dev(z + dz),
        dev(z + 2 * dz),
        dev(z - 2 * dz),
        dev(z + 3 * dz),
        y_partner,
        later,
        earlier,
    ]
    for friend in friends:
        pl.semaphore_signal(barrier, inc=1, device_id=friend, device_id_type=MESH)

    loads = {}
    for i, (name, src, dst) in enumerate(
        [
            ("ct", ct_h, ct),
            ("xf", xf_h, xf),
            ("wd", wd_h, wd),
            ("wg", wg_h, wg),
            ("wu", wu_h, wu),
            ("sg", sg_h, sg),
            ("su", su_h, su),
            ("xb", xb_h, xb),
        ]
    ):
        loads[name] = pltpu.make_async_copy(src, dst, ld.at[i])
        loads[name].start()

    def need(*names):
        for name in names:
            if name in loads:
                loads.pop(name).wait()

    copies = {}

    def remote(name, src, dst, s_sem, r_sem, target):
        copies[name] = pltpu.make_async_remote_copy(
            src_ref=src, dst_ref=dst, send_sem=s_sem, recv_sem=r_sem,
            device_id=target, device_id_type=MESH,
        )

    part = FF // W_PARTS
    for i in range(W_PARTS):
        cut = pl.ds(i * part, part)
        remote(f"W{i}", wd_h.at[cut, :], wdo.at[cut, :], s_w.at[i], r_w.at[i], y_partner)
    for name, block, out, s_sem, r_sem in (("C", csend, crow, s_c, r_c), ("F", fsend, frow, s_f, r_f)):
        for k in (1, 2, 3):
            remote(
                f"{name}{k}", rows(block, k), rows(out, place(k)), s_sem.at[k], r_sem.at[k], dev(targets[k])
            )
        for k in range(4):
            remote(
                f"{name}{4 + k}", rows(out, place(k)), rows(out, place(4 + k)),
                s_sem.at[4 + k], r_sem.at[4 + k], z_partner,
            )
    for j in range(8):
        if j - 4 in Y_BY_Z:
            remote(
                f"Y{j}", rows(frow, 8 + place(j - 4)), rows(frow, 8 + place(j)), s_y.at[j], r_y.at[j], z_partner
            )
        else:
            remote(f"Y{j}", rows(frow, place(j)), rows(frow, 8 + place(j)), s_y.at[j], r_y.at[j], y_partner)
        if j - 4 in G_BY_Z:
            remote(f"G{j}", rows(bsend, place(j)), rows(gadd, j - 4), s_g.at[j], r_g.at[j], z_partner)
        else:
            remote(f"G{j}", rows(bsend, place(j)), rows(brecv, place(j)), s_g.at[j], r_g.at[j], y_partner)
    remote("D", dsend, drecv, s_d.at[0], r_d.at[0], y_partner)
    for k in range(4):
        remote(f"H{k}", rows(hsend, 2 * k, 2), rows(hrecv, 2 * k, 2), s_h.at[k], r_h.at[k], y_partner)
        remote(f"BP{k}", rows(zsb, k), rows(zrb, k), s_bp.at[k], r_bp.at[k], z_partner)
        remote(f"FP{k}", rows(zsf, k), rows(zrf, k), s_fp.at[k], r_fp.at[k], z_partner)
    for k in (1, 2, 3):
        remote(f"BD{k}", rows(zdb, k), rows(retb, k), s_bd.at[k], r_bd.at[k], dev(sources[k]))
        remote(f"FD{k}", rows(zdf, k), rows(retf, k), s_fd.at[k], r_fd.at[k], dev(sources[k]))
    remote("RF", fout, nxt, s_out.at[0], r_out.at[0], later)
    remote("RB", gout, prv, s_out.at[1], r_out.at[1], earlier)

    computed = {}

    def compute(name, function, *given):
        computed[name] = (function, given)

    def cotangent_blocks():
        masks = selection(bids[...], slot_experts)
        b_hot[...] = weigh(masks, jnp.ones((2, TOK), F32)).T.astype(BF16)
        gather = weigh(masks, bw[...].astype(F32)).astype(BF16)
        need("ct")
        for cs in CHUNKS:
            csend[:, cs] = dot(gather, ct[:, cs]).astype(BF16)
        crow[span(0), :] = csend[span(0), :]

    def forward_blocks():
        masks = selection(fids[...], slot_experts)
        gather = weigh(masks, jnp.ones((2, TOK), F32)).astype(BF16)
        f_hot[...] = weigh(masks, fw[...].astype(F32)).T.astype(BF16)
        need("xf")
        wide = xf[...].astype(F32)
        scale = lax.rsqrt(jnp.mean(wide * wide, axis=-1, keepdims=True) + EPS)
        fout[...] = (wide * scale * gain[...].astype(F32)).astype(BF16)
        for cs in CHUNKS:
            fsend[:, cs] = dot(gather, fout[:, cs]).astype(BF16)
        frow[span(0), :] = fsend[span(0), :]

    def enter():
        pl.semaphore_wait(barrier, len(friends))

    def own_d_hidden():
        need("wd")
        dho[...] = dot_nt(crow[...], wd[...])

    def other_d_hidden():
        dsend[...] = dot_nt(crow[...], wdo[...]).astype(BF16)

    def activation_grad(j, column, d_hidden):
        need("sg", "su")
        start = pl.multiple_of((block_z[j] * 2 + column) * CAP, CAP)
        gate_b = sg[pl.ds(start, CAP), :].astype(F32)
        up_b = su[pl.ds(start, CAP), :].astype(F32)
        sigmoid = jax.nn.sigmoid(gate_b)
        d_gate = d_hidden * up_b * sigmoid * (1.0 + gate_b * (1.0 - sigmoid))
        d_up = d_hidden * gate_b * sigmoid
        return d_gate.astype(BF16), d_up.astype(BF16)

    def own_activation():
        for j in range(8):
            js = span(place(j))
            dg[js, :], du[js, :] = activation_grad(j, y, dho[js, :])

    def other_gradient():
        need("wg", "wu")
        for j in range(8):
            js = span(place(j))
            ks = span(place(j), 1, FULL)
            dg[ks, :], du[ks, :] = activation_grad(j, 1 - y, drecv[js, :].astype(F32))
        for cs in CHUNKS:
            total = dot_nt(dg[FULL:, :], wg[cs, :]) + dot_nt(du[FULL:, :], wu[cs, :])
            bsend[:, cs] = total.astype(BF16)

    def own_gradient():
        need("wg", "wu")
        for cs in CHUNKS:
            bown[:, cs] = dot_nt(dg[0:FULL, :], wg[cs, :]) + dot_nt(du[0:FULL, :], wu[cs, :])

    def hidden(block):
        need("wg", "wu")
        gate = dot(block, wg[...])
        up = dot(block, wu[...])
        return (gate * jax.nn.sigmoid(gate) * up).astype(BF16)

    def own_hidden():
        hown[...] = hidden(frow[0:FULL, :])

    def other_hidden(k):
        hsend[span(2 * k, 2), :] = hidden(frow[span(2 * k, 2, FULL), :])

    def forward_partial(k):
        need("wd")
        ks = span(2 * k, 2)
        for cs in CHUNKS:
            total = dot(hown[ks, :], wd[:, cs]) + dot(hrecv[ks, :], wdo[:, cs])
            fown[span(k), cs] = total[0:CAP, :]
            zsf[span(k), cs] = total[CAP:, :].astype(BF16)

    def forward_sum(k):
        total = (fown[span(k), :] + zrf[span(k), :].astype(F32)).astype(BF16)
        out = zdf if k else retf
        out[span(k), :] = total

    def gradient_across(k):
        js = span(place(k))
        bsend[js, :] = (bsend[js, :].astype(F32) + gadd[span(k), :].astype(F32)).astype(BF16)

    def gradient_partial(k):
        js = span(place(4 + k))
        total = bown[js, :]
        if k not in G_BY_Z:
            total = total + brecv[js, :].astype(F32)
        zsb[span(k), :] = total.astype(BF16)

    def gradient_sum(k):
        js = span(place(k))
        total = bown[js, :] + brecv[js, :].astype(F32) + zrb[span(k), :].astype(F32)
        out = zdb if k else retb
        out[span(k), :] = total.astype(BF16)

    def forward_out():
        for cs in CHUNKS:
            fout[:, cs] = (xf[:, cs].astype(F32) + dot(f_hot[...], retf[:, cs])).astype(BF16)

    def gradient_out():
        need("xb")
        wide_b = xb[...].astype(F32)
        scale_b = lax.rsqrt(jnp.mean(wide_b * wide_b, axis=-1, keepdims=True) + EPS)
        gain_wide = gain[...].astype(F32)
        inner = jnp.zeros((TOK, 1), F32)
        for cs in CHUNKS:
            d_unit = dot(b_hot[...], retb[:, cs]) * gain_wide[:, cs]
            dn[:, cs] = d_unit
            inner = inner + jnp.sum(d_unit * (xb[:, cs].astype(F32) * scale_b), axis=-1, keepdims=True)
        inner = inner * (1.0 / D)
        for cs in CHUNKS:
            unit = xb[:, cs].astype(F32) * scale_b
            gout[:, cs] = (ct[:, cs].astype(F32) + scale_b * (dn[:, cs] - unit * inner)).astype(BF16)

    compute("enter", enter)
    compute("dhown", own_d_hidden)
    compute("dhoth", other_d_hidden)
    compute("actown", own_activation)
    compute("bs", other_gradient)
    compute("bown", own_gradient)
    compute("hown", own_hidden)
    compute("cf", forward_out)
    compute("cb", gradient_out)
    for k in range(4):
        compute(f"h{k}", other_hidden, k)
        compute(f"fo{k}", forward_partial, k)
        compute(f"fa{k}", forward_sum, k)
        compute(f"gs{k}", gradient_across, k)
        compute(f"ba{k}", gradient_partial, k)
        compute(f"bb{k}", gradient_sum, k)

    cotangent_blocks()
    forward_blocks()
    sent = []
    for step in ORDER:
        kind, name = step[0], step[1:]
        if kind == "~":
            function, given = computed[name]
            function(*given)
        elif name == "RF":
            if kind == "+":
                pl.when(p < 15)(copies[name].start)
            else:
                pl.when(p > 0)(copies[name].wait_recv)
        elif name == "RB":
            if kind == "+":
                pl.when(p > 0)(copies[name].start)
            else:
                pl.when(p < 15)(copies[name].wait_recv)
        elif kind == "+":
            copies[name].start()
            sent.append(name)
        else:
            copies[name].wait_recv()

    @pl.when(p == 0)
    def _():
        gout[...] = jnp.zeros_like(gout)
        zero = pltpu.make_async_copy(gout, nxt, ld.at[8])
        zero.start()
        zero.wait()

    @pl.when(p == 15)
    def _():
        fout[...] = jnp.zeros_like(fout)
        zero = pltpu.make_async_copy(fout, prv, ld.at[9])
        zero.start()
        zero.wait()

    for name in sent:
        copies[name].wait_send()
    pl.when(p < 15)(copies["RF"].wait_send)
    pl.when(p > 0)(copies["RB"].wait_send)


def hand_over(first, second, first_out, second_out, held, in_sem, out_sem):
    cut = TOK // 2
    steps = []
    for i, (src, dst) in enumerate(((first, first_out), (second, second_out))):
        for j in range(2):
            here = pl.ds(j * cut, cut)
            steps.append(
                (
                    pltpu.make_async_copy(src.at[here, :], held.at[i, here, :], in_sem.at[i, j]),
                    pltpu.make_async_copy(held.at[i, here, :], dst.at[here, :], out_sem.at[i, j]),
                )
            )
    for arrive, _ in steps:
        arrive.start()
    for arrive, leave in steps:
        arrive.wait()
        leave.start()
    for _, leave in steps:
        leave.wait()


def body(
    fwd_rows,
    fwd_experts,
    fwd_weight,
    back_rows,
    back_experts,
    back_weight,
    back_cotangent,
    norm_gain,
    w_gate,
    w_up,
    w_down,
    saved_gate,
    saved_up,
):
    vmem = pl.BlockSpec(memory_space=pltpu.VMEM)
    hbm = pl.BlockSpec(memory_space=pl.ANY)
    dma = pltpu.SemaphoreType.DMA
    out_shape = (jax.ShapeDtypeStruct((TOK, D), BF16), jax.ShapeDtypeStruct((TOK, D), BF16))

    def wide(count, kind=BF16):
        return pltpu.VMEM((count, D), kind)

    def narrow(count, kind=BF16):
        return pltpu.VMEM((count, FF), kind)

    outs = pl.pallas_call(
        kernel,
        out_shape=out_shape,
        in_specs=[vmem] * 5 + [hbm] * 8,
        out_specs=(hbm, hbm),
        scratch_shapes=[
            wide(TOK), wide(TOK), wide(TOK),
            narrow(D), narrow(D), wide(FF), wide(FF), narrow(512), narrow(512),
            wide(HALF), wide(HALF), wide(FULL), wide(2 * FULL),
            narrow(FULL, F32), narrow(FULL), narrow(FULL), narrow(512), narrow(512),
            wide(FULL), wide(FULL), wide(HALF), wide(FULL, F32), wide(HALF), wide(HALF), wide(HALF), wide(HALF),
            narrow(FULL), narrow(FULL), narrow(FULL), wide(HALF, F32), wide(HALF), wide(HALF), wide(HALF),
            wide(HALF),
            wide(TOK), wide(TOK), wide(TOK, F32),
            pltpu.VMEM((TOK, HALF), BF16), pltpu.VMEM((TOK, HALF), BF16),
            dma((10,)), dma((W_PARTS,)), dma((W_PARTS,)), dma((8,)), dma((8,)), dma((8,)), dma((8,)),
            dma((8,)), dma((8,)), dma((1,)), dma((1,)), dma((8,)), dma((8,)),
            dma((4,)), dma((4,)), dma((4,)), dma((4,)), dma((4,)), dma((4,)),
            dma((4,)), dma((4,)), dma((4,)), dma((4,)), dma((2,)), dma((2,)),
        ],
        compiler_params=pltpu.CompilerParams(
            collective_id=0, has_side_effects=True, vmem_limit_bytes=56 * 2**20
        ),
        cost_estimate=pl.CostEstimate(flops=5_700_000_000, bytes_accessed=10_000_000, transcendentals=400_000),
    )(
        fwd_experts[0].T,
        fwd_weight[0].T,
        back_experts[0].T,
        back_weight[0].T,
        norm_gain,
        fwd_rows[0],
        back_rows[0],
        back_cotangent[0],
        w_gate[0, 0],
        w_up[0, 0],
        w_down[0, 0],
        saved_gate[0, 0],
        saved_up[0, 0],
    )
    outs = pl.pallas_call(
        hand_over,
        out_shape=out_shape,
        in_specs=[hbm, hbm],
        out_specs=(hbm, hbm),
        scratch_shapes=[pltpu.VMEM((2, TOK, D), BF16), dma((2, 2)), dma((2, 2))],
        compiler_params=pltpu.CompilerParams(vmem_limit_bytes=56 * 2**20),
    )(*outs)
    return outs[0][None], outs[1][None]


def solution(mesh):
    rows3 = P("pipe", "expert", None)
    rows4 = P("pipe", "expert", None, None)
    placed = (rows3,) * 7 + (P("pipe", None),) + (rows4,) * 5
    return jax.shard_map(
        body,
        mesh=mesh,
        in_specs=placed,
        out_specs=(rows3, rows3),
        check_vma=False,
    )
```

```python
import jax
import jax.numpy as jnp
from jax import lax
from jax.experimental import pallas as pl
from jax.experimental.pallas import tpu as pltpu
from jax.sharding import PartitionSpec as P

MESH = pl.DeviceIdType.MESH
D = 3584
FF = 256
TOK = 64
CAP = 32
HALF = 128
FULL = 256
COLS = 512
CHUNKS = [slice(c, c + COLS) for c in range(0, D, COLS)]
W_PARTS = 8
Y_BY_Z = ()
G_BY_Z = (0,)
EPS = 1e-06
F32 = jnp.float32
BF16 = jnp.bfloat16

ORDER = [
    "~enter", "+C2", "+F1", "+F3", "+C1", "+W0", "+C4", "+W1", "+W2", "?C2", "+W3", "+C6", "?W0",
    "?F1", "+F5", "+W4", "+W5", "+C3", "?C6", "?F3", "+Y3", "+F7", "+W6", "?F5", "?W1", "?W2",
    "?C1", "+F2", "?W3", "+C5", "?W4", "+Y5", "?C3", "?W5", "?Y3", "+C7", "?F7", "?C4", "+Y1",
    "+W7", "+Y7", "+F4", "?F2", "+F6", "?C7", "?C5", "~dhown", "~actown", "?Y1", "~bown", "?Y5",
    "~ba0", "?W6", "~h1", "+H1", "?W7", "+BP0", "~dhoth", "+D", "?F4", "?F6", "~hown", "?Y7", "~h3",
    "+H3", "+Y2", "?H1", "~fo1", "+FP1", "?D", "~bs", "+G7", "+Y6", "?H3", "~fo3", "+FP3", "+G4",
    "?FP3", "?G7", "+G3", "~fa3", "+FD3", "~ba3", "+BP3", "?Y2", "?Y6", "~h2", "?FP1", "~fa1",
    "+H2", "+G5", "+G6", "?H2", "~fo2", "+Y0", "+FP2", "?G5", "~ba1", "?BP3", "+FD1", "+BP1", "+Y4",
    "?G6", "+G1", "?FP2", "~fa2", "~ba2", "+FD2", "?G3", "~bb3", "+BD3", "?G4", "?FD3", "+BP2",
    "?Y0", "?Y4", "~h0", "+H0", "+G2", "?H0", "?G1", "?FD2", "?BP1", "~gs0", "~bb1", "+G0", "+BD1",
    "~fo0", "+FP0", "?G2", "?BP2", "~bb2", "?FD1", "+BD2", "?BP0", "?FP0", "~fa0", "~cf", "+RF",
    "?G0", "~bb0", "?BD2", "?BD1", "?BD3", "~cb", "+RB", "?RB", "?RF"
]


def dot(left, right):
    return lax.dot_general(left, right, (((1,), (0,)), ((), ())), preferred_element_type=F32)


def dot_nt(left, right):
    return lax.dot_general(left, right, (((1,), (1,)), ((), ())), preferred_element_type=F32)


def place(slot):
    return 2 * (slot % 4) + slot // 4


def span(position, count=1, base=0):
    return slice(base + position * CAP, base + (position + count) * CAP)


def rows(ref, position, count=1):
    return ref.at[pl.ds(position * CAP, count * CAP), :]


def selection(ids, slot_experts):
    line = lax.broadcasted_iota(jnp.int32, (HALF, TOK), 0)
    slot = lax.shift_right_logical(line, 5)
    rank_of = (line & (CAP - 1)).astype(F32)
    expert = jnp.zeros((HALF, TOK), jnp.int32)
    for s, e in enumerate(slot_experts):
        expert = jnp.where(slot == s, e, expert)
    first = ids[0:1, :] == expert
    second = ids[1:2, :] == expert
    named = jnp.where(first | second, 1.0, 0.0)
    before = lax.broadcasted_iota(jnp.int32, (TOK, TOK), 0) < lax.broadcasted_iota(
        jnp.int32, (TOK, TOK), 1
    )
    ranks = dot(named.astype(BF16), jnp.where(before, 1.0, 0.0).astype(BF16))
    hit = ranks == rank_of
    return first & hit, second & hit


def weigh(masks, weights):
    first, second = masks
    return jnp.where(first, weights[0:1, :], 0.0) + jnp.where(second, weights[1:2, :], 0.0)


def kernel(
    fids, fw, bids, bw, gain, xf_h, xb_h, ct_h, wg_h, wu_h, wd_h, sg_h, su_h,
    nxt, prv,
    xf, xb, ct, wg, wu, wd, wdo, sg, su,
    csend, fsend, crow, frow,
    dho, dsend, drecv, dg, du,
    bsend, brecv, gadd, bown, zsb, zrb, zdb, retb,
    hown, hsend, hrecv, fown, zsf, zrf, zdf, retf,
    fout, gout, dn, b_hot, f_hot,
    ld, s_w, r_w, s_c, r_c, s_f, r_f, s_y, r_y, s_d, r_d, s_g, r_g,
    s_bp, r_bp, s_bd, r_bd, s_h, r_h, s_fp, r_fp, s_fd, r_fd, s_out, r_out,
):
    p = lax.axis_index("pipe")
    me = lax.axis_index("expert")
    z = lax.div(me, 2)
    y = lax.rem(me, 2)
    dz = 2 * lax.rem(z, 2) - 1

    def at_z(zz):
        return lax.rem(zz + 8, 8)

    def dev(zz):
        return (p, at_z(zz) * 2 + y)

    targets = [z, z + dz, z - 2 * dz, z + 3 * dz]
    sources = [z, z + dz, z + 2 * dz, z + 3 * dz]
    pz = z - dz
    z_partner = dev(pz)
    y_partner = (p, z * 2 + 1 - y)
    later = (lax.rem(p + 1, 16), me)
    earlier = (lax.rem(p + 15, 16), me)
    slot_experts = [lax.div(at_z(t), 2) for t in targets]
    block_z = [at_z(s) for s in sources] + [at_z(pz - k * dz) for k in range(4)]

    barrier = pltpu.get_barrier_semaphore()
    friends = [
        z_partner,
        dev(z + dz),
        dev(z + 2 * dz),
        dev(z - 2 * dz),
        dev(z + 3 * dz),
        y_partner,
        later,
        earlier,
    ]
    for friend in friends:
        pl.semaphore_signal(barrier, inc=1, device_id=friend, device_id_type=MESH)

    loads = {}
    for i, (name, src, dst) in enumerate(
        [
            ("ct", ct_h, ct),
            ("xf", xf_h, xf),
            ("wd", wd_h, wd),
            ("wg", wg_h, wg),
            ("wu", wu_h, wu),
            ("sg", sg_h, sg),
            ("su", su_h, su),
            ("xb", xb_h, xb),
        ]
    ):
        loads[name] = pltpu.make_async_copy(src, dst, ld.at[i])
        loads[name].start()

    def need(*names):
        for name in names:
            if name in loads:
                loads.pop(name).wait()

    copies = {}

    def remote(name, src, dst, s_sem, r_sem, target):
        copies[name] = pltpu.make_async_remote_copy(
            src_ref=src, dst_ref=dst, send_sem=s_sem, recv_sem=r_sem,
            device_id=target, device_id_type=MESH,
        )

    part = FF // W_PARTS
    for i in range(W_PARTS):
        cut = pl.ds(i * part, part)
        remote(f"W{i}", wd_h.at[cut, :], wdo.at[cut, :], s_w.at[i], r_w.at[i], y_partner)
    for name, block, out, s_sem, r_sem in (("C", csend, crow, s_c, r_c), ("F", fsend, frow, s_f, r_f)):
        for k in (1, 2, 3):
            remote(
                f"{name}{k}", rows(block, k), rows(out, place(k)), s_sem.at[k], r_sem.at[k], dev(targets[k])
            )
        for k in range(4):
            remote(
                f"{name}{4 + k}", rows(out, place(k)), rows(out, place(4 + k)),
                s_sem.at[4 + k], r_sem.at[4 + k], z_partner,
            )
    for j in range(8):
        if j - 4 in Y_BY_Z:
            remote(
                f"Y{j}", rows(frow, 8 + place(j - 4)), rows(frow, 8 + place(j)), s_y.at[j], r_y.at[j], z_partner
            )
        else:
            remote(f"Y{j}", rows(frow, place(j)), rows(frow, 8 + place(j)), s_y.at[j], r_y.at[j], y_partner)
        if j - 4 in G_BY_Z:
            remote(f"G{j}", rows(bsend, place(j)), rows(gadd, j - 4), s_g.at[j], r_g.at[j], z_partner)
        else:
            remote(f"G{j}", rows(bsend, place(j)), rows(brecv, place(j)), s_g.at[j], r_g.at[j], y_partner)
    remote("D", dsend, drecv, s_d.at[0], r_d.at[0], y_partner)
    for k in range(4):
        remote(f"H{k}", rows(hsend, 2 * k, 2), rows(hrecv, 2 * k, 2), s_h.at[k], r_h.at[k], y_partner)
        remote(f"BP{k}", rows(zsb, k), rows(zrb, k), s_bp.at[k], r_bp.at[k], z_partner)
        remote(f"FP{k}", rows(zsf, k), rows(zrf, k), s_fp.at[k], r_fp.at[k], z_partner)
    for k in (1, 2, 3):
        remote(f"BD{k}", rows(zdb, k), rows(retb, k), s_bd.at[k], r_bd.at[k], dev(sources[k]))
        remote(f"FD{k}", rows(zdf, k), rows(retf, k), s_fd.at[k], r_fd.at[k], dev(sources[k]))
    for h in range(2):
        remote(f"RF{h}", rows(fout, h), rows(nxt, h), s_out.at[h], r_out.at[h], later)
        remote(f"RB{h}", rows(gout, h), rows(prv, h), s_out.at[2 + h], r_out.at[2 + h], earlier)

    computed = {}

    def compute(name, function, *given):
        computed[name] = (function, given)

    def cotangent_blocks():
        masks = selection(bids[...], slot_experts)
        b_hot[...] = weigh(masks, jnp.ones((2, TOK), F32)).T.astype(BF16)
        gather = weigh(masks, bw[...].astype(F32)).astype(BF16)
        need("ct")
        for cs in CHUNKS:
            csend[:, cs] = dot(gather, ct[:, cs]).astype(BF16)
        crow[span(0), :] = csend[span(0), :]

    def forward_blocks():
        masks = selection(fids[...], slot_experts)
        gather = weigh(masks, jnp.ones((2, TOK), F32)).astype(BF16)
        f_hot[...] = weigh(masks, fw[...].astype(F32)).T.astype(BF16)
        need("xf")
        wide = xf[...].astype(F32)
        scale = lax.rsqrt(jnp.mean(wide * wide, axis=-1, keepdims=True) + EPS)
        fout[...] = (wide * scale * gain[...].astype(F32)).astype(BF16)
        for cs in CHUNKS:
            fsend[:, cs] = dot(gather, fout[:, cs]).astype(BF16)
        frow[span(0), :] = fsend[span(0), :]

    def enter():
        pl.semaphore_wait(barrier, len(friends))

    def own_d_hidden():
        need("wd")
        dho[...] = dot_nt(crow[...], wd[...])

    def other_d_hidden():
        dsend[...] = dot_nt(crow[...], wdo[...]).astype(BF16)

    def activation_grad(j, column, d_hidden):
        need("sg", "su")
        start = pl.multiple_of((block_z[j] * 2 + column) * CAP, CAP)
        gate_b = sg[pl.ds(start, CAP), :].astype(F32)
        up_b = su[pl.ds(start, CAP), :].astype(F32)
        sigmoid = jax.nn.sigmoid(gate_b)
        d_gate = d_hidden * up_b * sigmoid * (1.0 + gate_b * (1.0 - sigmoid))
        d_up = d_hidden * gate_b * sigmoid
        return d_gate.astype(BF16), d_up.astype(BF16)

    def own_activation():
        for j in range(8):
            js = span(place(j))
            dg[js, :], du[js, :] = activation_grad(j, y, dho[js, :])

    def other_gradient():
        need("wg", "wu")
        for j in range(8):
            js = span(place(j))
            ks = span(place(j), 1, FULL)
            dg[ks, :], du[ks, :] = activation_grad(j, 1 - y, drecv[js, :].astype(F32))
        for cs in CHUNKS:
            total = dot_nt(dg[FULL:, :], wg[cs, :]) + dot_nt(du[FULL:, :], wu[cs, :])
            bsend[:, cs] = total.astype(BF16)

    def own_gradient():
        need("wg", "wu")
        for cs in CHUNKS:
            bown[:, cs] = dot_nt(dg[0:FULL, :], wg[cs, :]) + dot_nt(du[0:FULL, :], wu[cs, :])

    def hidden(block):
        need("wg", "wu")
        gate = dot(block, wg[...])
        up = dot(block, wu[...])
        return (gate * jax.nn.sigmoid(gate) * up).astype(BF16)

    def own_hidden():
        hown[...] = hidden(frow[0:FULL, :])

    def other_hidden(k):
        hsend[span(2 * k, 2), :] = hidden(frow[span(2 * k, 2, FULL), :])

    def forward_partial(k):
        need("wd")
        ks = span(2 * k, 2)
        for cs in CHUNKS:
            total = dot(hown[ks, :], wd[:, cs]) + dot(hrecv[ks, :], wdo[:, cs])
            fown[span(k), cs] = total[0:CAP, :]
            zsf[span(k), cs] = total[CAP:, :].astype(BF16)

    def forward_sum(k):
        total = (fown[span(k), :] + zrf[span(k), :].astype(F32)).astype(BF16)
        out = zdf if k else retf
        out[span(k), :] = total

    def gradient_across(k):
        js = span(place(k))
        bsend[js, :] = (bsend[js, :].astype(F32) + gadd[span(k), :].astype(F32)).astype(BF16)

    def gradient_partial(k):
        js = span(place(4 + k))
        total = bown[js, :]
        if k not in G_BY_Z:
            total = total + brecv[js, :].astype(F32)
        zsb[span(k), :] = total.astype(BF16)

    def gradient_sum(k):
        js = span(place(k))
        total = bown[js, :] + brecv[js, :].astype(F32) + zrb[span(k), :].astype(F32)
        out = zdb if k else retb
        out[span(k), :] = total.astype(BF16)

    def forward_out(h):
        hs = span(h)
        for cs in CHUNKS:
            fout[hs, cs] = (xf[hs, cs].astype(F32) + dot(f_hot[hs, :], retf[:, cs])).astype(BF16)

    def gradient_out(h):
        need("xb")
        hs = span(h)
        wide_b = xb[hs, :].astype(F32)
        scale_b = lax.rsqrt(jnp.mean(wide_b * wide_b, axis=-1, keepdims=True) + EPS)
        gain_wide = gain[...].astype(F32)
        inner = jnp.zeros((CAP, 1), F32)
        for cs in CHUNKS:
            d_unit = dot(b_hot[hs, :], retb[:, cs]) * gain_wide[:, cs]
            dn[hs, cs] = d_unit
            inner = inner + jnp.sum(d_unit * (xb[hs, cs].astype(F32) * scale_b), axis=-1, keepdims=True)
        inner = inner * (1.0 / D)
        for cs in CHUNKS:
            unit = xb[hs, cs].astype(F32) * scale_b
            gout[hs, cs] = (ct[hs, cs].astype(F32) + scale_b * (dn[hs, cs] - unit * inner)).astype(BF16)

    compute("enter", enter)
    compute("dhown", own_d_hidden)
    compute("dhoth", other_d_hidden)
    compute("actown", own_activation)
    compute("bs", other_gradient)
    compute("bown", own_gradient)
    compute("hown", own_hidden)
    compute("cf", forward_out, 0)
    compute("cb", gradient_out, 0)
    for k in range(4):
        compute(f"h{k}", other_hidden, k)
        compute(f"fo{k}", forward_partial, k)
        compute(f"fa{k}", forward_sum, k)
        compute(f"gs{k}", gradient_across, k)
        compute(f"ba{k}", gradient_partial, k)
        compute(f"bb{k}", gradient_sum, k)

    cotangent_blocks()
    forward_blocks()
    sent = []
    for step in ORDER:
        kind, name = step[0], step[1:]
        if kind == "~":
            function, given = computed[name]
            function(*given)
        elif name == "RF":
            if kind == "+":
                pl.when(p < 15)(copies["RF0"].start)
                forward_out(1)
                pl.when(p < 15)(copies["RF1"].start)
            else:
                for h in range(2):
                    pl.when(p > 0)(copies[f"RF{h}"].wait_recv)
        elif name == "RB":
            if kind == "+":
                pl.when(p > 0)(copies["RB0"].start)
                gradient_out(1)
                pl.when(p > 0)(copies["RB1"].start)
            else:
                for h in range(2):
                    pl.when(p < 15)(copies[f"RB{h}"].wait_recv)
        elif kind == "+":
            copies[name].start()
            sent.append(name)
        else:
            copies[name].wait_recv()

    @pl.when(p == 0)
    def _():
        gout[...] = jnp.zeros_like(gout)
        zero = pltpu.make_async_copy(gout, nxt, ld.at[8])
        zero.start()
        zero.wait()

    @pl.when(p == 15)
    def _():
        fout[...] = jnp.zeros_like(fout)
        zero = pltpu.make_async_copy(fout, prv, ld.at[9])
        zero.start()
        zero.wait()

    for name in sent:
        copies[name].wait_send()
    for h in range(2):
        pl.when(p < 15)(copies[f"RF{h}"].wait_send)
        pl.when(p > 0)(copies[f"RB{h}"].wait_send)


def hand_over(first, second, first_out, second_out, held, in_sem, out_sem):
    cut = TOK // 2
    steps = []
    for i, (src, dst) in enumerate(((first, first_out), (second, second_out))):
        for j in range(2):
            here = pl.ds(j * cut, cut)
            steps.append(
                (
                    pltpu.make_async_copy(src.at[here, :], held.at[i, here, :], in_sem.at[i, j]),
                    pltpu.make_async_copy(held.at[i, here, :], dst.at[here, :], out_sem.at[i, j]),
                )
            )
    for arrive, _ in steps:
        arrive.start()
    for arrive, leave in steps:
        arrive.wait()
        leave.start()
    for _, leave in steps:
        leave.wait()


def body(
    fwd_rows,
    fwd_experts,
    fwd_weight,
    back_rows,
    back_experts,
    back_weight,
    back_cotangent,
    norm_gain,
    w_gate,
    w_up,
    w_down,
    saved_gate,
    saved_up,
):
    vmem = pl.BlockSpec(memory_space=pltpu.VMEM)
    hbm = pl.BlockSpec(memory_space=pl.ANY)
    dma = pltpu.SemaphoreType.DMA
    out_shape = (jax.ShapeDtypeStruct((TOK, D), BF16), jax.ShapeDtypeStruct((TOK, D), BF16))

    def wide(count, kind=BF16):
        return pltpu.VMEM((count, D), kind)

    def narrow(count, kind=BF16):
        return pltpu.VMEM((count, FF), kind)

    outs = pl.pallas_call(
        kernel,
        out_shape=out_shape,
        in_specs=[vmem] * 5 + [hbm] * 8,
        out_specs=(hbm, hbm),
        scratch_shapes=[
            wide(TOK), wide(TOK), wide(TOK),
            narrow(D), narrow(D), wide(FF), wide(FF), narrow(512), narrow(512),
            wide(HALF), wide(HALF), wide(FULL), wide(2 * FULL),
            narrow(FULL, F32), narrow(FULL), narrow(FULL), narrow(512), narrow(512),
            wide(FULL), wide(FULL), wide(HALF), wide(FULL, F32), wide(HALF), wide(HALF), wide(HALF), wide(HALF),
            narrow(FULL), narrow(FULL), narrow(FULL), wide(HALF, F32), wide(HALF), wide(HALF), wide(HALF),
            wide(HALF),
            wide(TOK), wide(TOK), wide(TOK, F32),
            pltpu.VMEM((TOK, HALF), BF16), pltpu.VMEM((TOK, HALF), BF16),
            dma((10,)), dma((W_PARTS,)), dma((W_PARTS,)), dma((8,)), dma((8,)), dma((8,)), dma((8,)),
            dma((8,)), dma((8,)), dma((1,)), dma((1,)), dma((8,)), dma((8,)),
            dma((4,)), dma((4,)), dma((4,)), dma((4,)), dma((4,)), dma((4,)),
            dma((4,)), dma((4,)), dma((4,)), dma((4,)), dma((4,)), dma((4,)),
        ],
        compiler_params=pltpu.CompilerParams(
            collective_id=0, has_side_effects=True, vmem_limit_bytes=56 * 2**20
        ),
        cost_estimate=pl.CostEstimate(flops=5_700_000_000, bytes_accessed=10_000_000, transcendentals=400_000),
    )(
        fwd_experts[0].T,
        fwd_weight[0].T,
        back_experts[0].T,
        back_weight[0].T,
        norm_gain,
        fwd_rows[0],
        back_rows[0],
        back_cotangent[0],
        w_gate[0, 0],
        w_up[0, 0],
        w_down[0, 0],
        saved_gate[0, 0],
        saved_up[0, 0],
    )
    outs = pl.pallas_call(
        hand_over,
        out_shape=out_shape,
        in_specs=[hbm, hbm],
        out_specs=(hbm, hbm),
        scratch_shapes=[pltpu.VMEM((2, TOK, D), BF16), dma((2, 2)), dma((2, 2))],
        compiler_params=pltpu.CompilerParams(vmem_limit_bytes=56 * 2**20),
    )(*outs)
    return outs[0][None], outs[1][None]


def solution(mesh):
    rows3 = P("pipe", "expert", None)
    rows4 = P("pipe", "expert", None, None)
    placed = (rows3,) * 7 + (P("pipe", None),) + (rows4,) * 5
    return jax.shard_map(
        body,
        mesh=mesh,
        in_specs=placed,
        out_specs=(rows3, rows3),
        check_vma=False,
    )
```
